256 devices in a mesh: tower: 2 (over z_hi), dp: 128 (over z_lo, x, y, core).
Axes of the slice: x: 4, y: 4, z: 8 (z_hi: 2, z_lo: 4; z = z_hi * 4 + z_lo), core: 2. Of those that a mesh axis runs over, the one named last changes fastest.
Arguments:
- picture_encoder_summary_vector: bfloat16 [8192, 1664], P('dp', 'tower'), may hold values from -6 to 6
- caption_encoder_summary_vector: bfloat16 [8192, 1280], P('dp', 'tower'), may hold values from -6 to 6
- picture_closing_norm_multiplier: float32 [1664], P('tower'), may hold values from 0.5 to 1.5
- caption_closing_norm_multiplier: float32 [1280], P('tower'), may hold values from 0.5 to 1.5
- picture_embedding_matrix: bfloat16 [1664, 1280], P('tower'), may hold values from -0.15625 to 0.15625
- caption_embedding_matrix: bfloat16 [1280, 1280], P('tower'), may hold values from -0.15625 to 0.15625
- similarity_sharpness: float32 [1], replicated, may hold values from 20 to 80
- similarity_offset: float32 [1], replicated, may hold values from -8 to -4
Outputs:
- image_proj_grad: float32 [1664, 1280], P('tower')
- text_proj_grad: float32 [1280, 1280], P('tower')
The draws below stay inside these ranges and needn't reach their ends.
All inputs are finite; a program needn't handle non-finite values.
Results may differ from the reference program's by a relative error of at most 0.004.
Values may be sent and summed in bfloat16 or wider, within the bound.
No kernel may reach another device: no remote copies, remote signals or barrier semaphores. Data moves between devices by JAX's collectives and lax.ppermute only.
A program may use at most 128 MiB of HBM per device.

```python
import math
import jax
import jax.numpy as jnp
from jax import lax

DI = 1664
DT = 1280
EMB = 1280
BATCH = 8192


def shard_levels(key, extent, shards, low, top_value):
    level = 1.0
    for position, shards_of in shards:
        draws = jax.random.uniform(jax.random.fold_in(jax.random.fold_in(key, 6), position), (shards_of,), jnp.float32, low / len(shards), top_value / len(shards))
        level = level * jnp.repeat(jnp.exp(draws), extent[position] // shards_of).reshape((-1,) + (1,) * (len(extent) - 1 - position))
    return level


def centred(own_key, shape, scale, bound, cuts=(), kind=jnp.bfloat16):
    level = shard_levels(own_key, shape, cuts, -0.22, 0.18) if cuts else 1.0
    array = jax.random.normal(own_key, shape, jnp.float32) * scale * level
    return jnp.minimum(jnp.maximum(array, -bound), bound).astype(kind)


def setup_inputs(seed: int = 0) -> dict:
    key_of = jax.random.split(jax.random.key(seed), 9)
    picture_encoder_summary_vector = centred(key_of[0], (BATCH, DI), 1.0, 6.0, ((0, 128), (1, 2)))
    caption_encoder_summary_vector = centred(key_of[1], (BATCH, DT), 1.0, 6.0, ((0, 128), (1, 2)))
    picture_closing_norm_multiplier = jnp.clip(1.0 + 0.1 * jax.random.normal(key_of[2], (DI,), jnp.float32), 0.5, 1.5)
    caption_closing_norm_multiplier = jnp.clip(1.0 + 0.1 * jax.random.normal(key_of[3], (DT,), jnp.float32), 0.5, 1.5)
    picture_embedding_matrix = centred(key_of[4], (DI, EMB), DI ** -0.5, 0.15625, ((0, 2),))
    caption_embedding_matrix = centred(key_of[5], (DT, EMB), DT ** -0.5, 0.15625, ((0, 2),))
    similarity_sharpness = jnp.clip(jnp.exp(jax.random.uniform(key_of[6], (1,), jnp.float32, math.log(20.0), math.log(80.0))), 20.0, 80.0)
    similarity_offset = jnp.clip(jax.random.uniform(key_of[7], (1,), jnp.float32, -8.0, -4.0), -8.0, -4.0)
    return dict(picture_encoder_summary_vector=picture_encoder_summary_vector, caption_encoder_summary_vector=caption_encoder_summary_vector, picture_closing_norm_multiplier=picture_closing_norm_multiplier, caption_closing_norm_multiplier=caption_closing_norm_multiplier, picture_embedding_matrix=picture_embedding_matrix, caption_embedding_matrix=caption_embedding_matrix, similarity_sharpness=similarity_sharpness, similarity_offset=similarity_offset)


def layer_normed(features, gain):
    values = features.astype(jnp.float32)
    average = lax.optimization_barrier(jnp.mean(values, axis=1, keepdims=True))
    squares = lax.optimization_barrier(jnp.mean(values * values, axis=1, keepdims=True))
    inverse = lax.rsqrt(squares - average * average + 1e-06)
    return ((values - average) * inverse * gain[None, :]).astype(jnp.bfloat16)

def unit_rows(projected):
    length = jnp.sqrt(lax.optimization_barrier(jnp.sum(projected * projected, axis=1, keepdims=True)) + 1e-06)
    return (projected / length, length)

def pair_gradient(own_rows, other_rows, similarity_multiplier, bias_value):
    block_size = math.gcd(own_rows.shape[0], 512)
    block_count = own_rows.shape[0] // block_size
    blocks = own_rows.reshape(block_count, block_size, own_rows.shape[1])
    offsets = jnp.arange(block_count, dtype=jnp.int32) * block_size

    def one_block(inputs):
        block_rows, offset = inputs
        products = lax.dot_general(block_rows, other_rows, (((1,), (1,)), ((), ())), preferred_element_type=jnp.float32)
        logits = similarity_multiplier * products + bias_value
        row_ids = offset + lax.broadcasted_iota(jnp.int32, products.shape, 0)
        col_ids = lax.broadcasted_iota(jnp.int32, products.shape, 1)
        labels = jnp.where(row_ids == col_ids, 1.0, -1.0).astype(jnp.float32)
        weights = (-labels * jax.nn.sigmoid(-labels * logits)).astype(jnp.bfloat16)
        return jnp.dot(weights, other_rows, preferred_element_type=jnp.float32)
    summed = lax.map(one_block, (blocks, offsets))
    return similarity_multiplier * summed.reshape(own_rows.shape[0], other_rows.shape[1])

def pre_gradient(unit, length, gradient):
    along = lax.optimization_barrier(jnp.sum(unit * gradient, axis=1, keepdims=True))
    return ((gradient - unit * along) / length).astype(jnp.bfloat16)

def reference(picture_encoder_summary_vector, caption_encoder_summary_vector, picture_closing_norm_multiplier, caption_closing_norm_multiplier, picture_embedding_matrix, caption_embedding_matrix, similarity_sharpness, similarity_offset):
    similarity_multiplier = similarity_sharpness[0]
    bias_value = similarity_offset[0]
    image_normed = layer_normed(picture_encoder_summary_vector, picture_closing_norm_multiplier)
    text_normed = layer_normed(caption_encoder_summary_vector, caption_closing_norm_multiplier)
    image_unit, image_length = unit_rows(jnp.dot(image_normed, picture_embedding_matrix, preferred_element_type=jnp.float32))
    text_unit, text_length = unit_rows(jnp.dot(text_normed, caption_embedding_matrix, preferred_element_type=jnp.float32))
    image_embed = image_unit.astype(jnp.bfloat16)
    text_embed = text_unit.astype(jnp.bfloat16)
    image_grad = pair_gradient(image_embed, text_embed, similarity_multiplier, bias_value)
    text_grad = pair_gradient(text_embed, image_embed, similarity_multiplier, bias_value)
    image_slope = pre_gradient(image_unit, image_length, image_grad)
    text_slope = pre_gradient(text_unit, text_length, text_grad)
    image_proj_grad = lax.dot_general(image_normed, image_slope, (((0,), (0,)), ((), ())), preferred_element_type=jnp.float32)
    text_proj_grad = lax.dot_general(text_normed, text_slope, (((0,), (0,)), ((), ())), preferred_element_type=jnp.float32)
    return (image_proj_grad, text_proj_grad)
```

```python
import jax
import jax.numpy as jnp
from jax import lax
from jax.sharding import Mesh, PartitionSpec as P

AXES = ("t", "z", "x", "y", "c")
DP = ("z", "x", "y", "c")


def swap(x, axis, mask=1):
    return lax.ppermute(x, axis, [(i, i ^ mask) for i in range(lax.axis_size(axis))])


def normed_half(values, sums, squares, width, gain):
    average = (sums / width)[:, None]
    inverse = lax.rsqrt((squares / width)[:, None] - average * average + 1e-06)
    return ((values - average) * inverse * gain[None, :]).astype(jnp.bfloat16)


def split3(x):
    high = x.astype(jnp.bfloat16)
    rest = x - high.astype(jnp.float32)
    mid = rest.astype(jnp.bfloat16)
    low = (rest - mid.astype(jnp.float32)).astype(jnp.bfloat16)
    column = lax.broadcasted_iota(jnp.int32, (x.shape[0], 128), 1)
    zero = jnp.zeros((), jnp.bfloat16)
    return jnp.where(
        column == 0, high, jnp.where(column == 1, mid, jnp.where(column == 2, low, zero))
    )


def packed_rows(projected):
    length = jnp.sqrt(jnp.sum(projected * projected, axis=1, keepdims=True) + 1e-06)
    unit = (projected / length).astype(jnp.bfloat16)
    return jnp.concatenate([unit, split3(length)], axis=1)


def gather_xy(x):
    x = lax.all_gather(x, "y", axis=0, tiled=True)
    return lax.all_gather(x, "x", axis=0, tiled=True)


def gather_zc(x):
    x = lax.all_gather(x, "z", axis=0, tiled=True)
    other = swap(x, "c")
    first = lax.axis_index("c") == 0
    return jnp.concatenate([jnp.where(first, x, other), jnp.where(first, other, x)], axis=0)


def slope(gradient, packed, width):
    unit = packed[:, :width].astype(jnp.float32)
    length = jnp.sum(packed[:, width:].astype(jnp.float32), axis=1, keepdims=True)
    along = jnp.sum(unit * gradient, axis=1, keepdims=True)
    return ((gradient - unit * along) / length).astype(jnp.bfloat16)


def per_device(image_x, text_x, image_gain, text_gain, image_w, text_w, sharpness, offset):
    scale, bias = sharpness[0], offset[0]
    towers = lax.axis_size("t")
    rows, width = image_x.shape[0], image_w.shape[1]
    image_values = image_x.astype(jnp.float32)
    text_values = text_x.astype(jnp.float32)
    moments = lax.psum(
        (
            jnp.sum(image_values, axis=1),
            jnp.sum(image_values * image_values, axis=1),
            jnp.sum(text_values, axis=1),
            jnp.sum(text_values * text_values, axis=1),
        ),
        "t",
    )
    image_normed = normed_half(
        image_values, moments[0], moments[1], image_x.shape[1] * towers, image_gain
    )
    text_normed = normed_half(
        text_values, moments[2], moments[3], text_x.shape[1] * towers, text_gain
    )
    image_part = jnp.dot(image_normed, image_w, preferred_element_type=jnp.float32)
    text_part = jnp.dot(text_normed, text_w, preferred_element_type=jnp.float32)
    image_pre = image_part + swap(image_part.astype(jnp.bfloat16), "t").astype(jnp.float32)
    text_pre = text_part + swap(text_part.astype(jnp.bfloat16), "t").astype(jnp.float32)
    image_rows = gather_xy(packed_rows(image_pre))
    text_rows = gather_zc(packed_rows(text_pre))
    image_normed_rows = gather_xy(image_normed)
    text_normed_rows = gather_zc(text_normed)

    image_units, text_units = image_rows[:, :width], text_rows[:, :width]
    products = lax.dot_general(
        image_units, text_units, (((1,), (1,)), ((), ())), preferred_element_type=jnp.float32
    )
    logits = scale * products + bias
    sizes = {axis: lax.axis_size(axis) for axis in DP}
    own_image = (lax.axis_index("x") * sizes["y"] + lax.axis_index("y")) * rows
    own_text = (lax.axis_index("c") * sizes["z"] + lax.axis_index("z")) * rows
    row_ids = lax.broadcasted_iota(jnp.int32, products.shape, 0) - own_image
    column_ids = lax.broadcasted_iota(jnp.int32, products.shape, 1) - own_text
    same = (row_ids == column_ids) & (row_ids >= 0) & (row_ids < rows)
    labels = jnp.where(same, 1.0, -1.0).astype(jnp.float32)
    weights = (-labels * jax.nn.sigmoid(-labels * logits)).astype(jnp.bfloat16)
    image_grad = scale * jnp.dot(weights, text_units, preferred_element_type=jnp.float32)
    text_grad = scale * lax.dot_general(
        weights, image_units, (((0,), (0,)), ((), ())), preferred_element_type=jnp.float32
    )
    image_slope = slope(image_grad, image_rows, width)
    text_slope = slope(text_grad, text_rows, width)
    image_term = lax.dot_general(
        image_normed_rows, image_slope, (((0,), (0,)), ((), ())), preferred_element_type=jnp.float32
    )
    text_term = lax.dot_general(
        text_normed_rows, text_slope, (((0,), (0,)), ((), ())), preferred_element_type=jnp.float32
    )
    term = jnp.concatenate([image_term, text_term], axis=0)
    half = width // 2
    first = lax.axis_index("c") == 0
    kept = jnp.where(first, term[:, :half], term[:, half:])
    sent = jnp.where(first, term[:, half:], term[:, :half])
    kept = (kept + swap(sent, "c")).astype(jnp.bfloat16)
    groups = sizes["x"] * sizes["y"]
    blocks = kept.reshape(groups, kept.shape[0] // groups, half)
    blocks = lax.all_to_all(blocks, ("x", "y"), 0, 0)
    block = jnp.sum(blocks.astype(jnp.float32), axis=0).astype(jnp.bfloat16)
    others = [swap(block, "z", k).astype(jnp.float32) for k in range(1, sizes["z"])]
    block = (block.astype(jnp.float32) + others[0]) + (others[1] + others[2])
    block = block.astype(jnp.bfloat16)[None]
    block = gather_xy(block).reshape(kept.shape)
    other = swap(block, "c")
    full = jnp.concatenate(
        [jnp.where(first, block, other), jnp.where(first, other, block)], axis=1
    ).astype(jnp.float32)
    depth = image_w.shape[0]
    return full[:depth], full[depth:]


def solution(mesh):
    grid = Mesh(mesh.devices.reshape(2, 4, 4, 4, 2), AXES)
    return jax.shard_map(
        per_device,
        mesh=grid,
        in_specs=(
            P(DP, "t"),
            P(DP, "t"),
            P("t"),
            P("t"),
            P("t", None),
            P("t", None),
            P(),
            P(),
        ),
        out_specs=(P("t", None), P("t", None)),
        check_vma=False,
    )
```

```python
import jax
import jax.numpy as jnp
from jax import lax
from jax.sharding import Mesh, PartitionSpec as P

AXES = ("t", "z", "x", "y", "c")
DP = ("z", "x", "y", "c")


def swap(x, axis, mask=1):
    return lax.ppermute(x, axis, [(i, i ^ mask) for i in range(lax.axis_size(axis))])


def normed_half(values, sums, squares, width, gain):
    average = (sums / width)[:, None]
    inverse = lax.rsqrt((squares / width)[:, None] - average * average + 1e-06)
    return ((values - average) * inverse * gain[None, :]).astype(jnp.bfloat16)


def split3(x):
    high = x.astype(jnp.bfloat16)
    rest = x - high.astype(jnp.float32)
    mid = rest.astype(jnp.bfloat16)
    low = (rest - mid.astype(jnp.float32)).astype(jnp.bfloat16)
    column = lax.broadcasted_iota(jnp.int32, (x.shape[0], 128), 1)
    zero = jnp.zeros((), jnp.bfloat16)
    return jnp.where(
        column == 0, high, jnp.where(column == 1, mid, jnp.where(column == 2, low, zero))
    )


def packed_rows(projected):
    length = jnp.sqrt(jnp.sum(projected * projected, axis=1, keepdims=True) + 1e-06)
    unit = (projected / length).astype(jnp.bfloat16)
    return jnp.concatenate([unit, split3(length)], axis=1)


PATHS = (
    (("x", 1), ("x", 3), ("y", 1), ("y", 3)),
    (("x", 3), ("x", 1), ("y", 3), ("y", 1)),
    (("y", 1), ("y", 3), ("x", 1), ("x", 3)),
    (("y", 3), ("y", 1), ("x", 3), ("x", 1)),
)


def gather_xy(x):
    parts = jnp.split(x, len(PATHS), axis=0)
    for step in range(len(PATHS[0])):
        parts = [
            jnp.concatenate([part, swap(part, *path[step])], axis=0)
            for part, path in zip(parts, PATHS)
        ]
    return jnp.concatenate(parts, axis=0)


def gather_zc(x):
    x = jnp.concatenate([x] + [swap(x, "z", k) for k in range(1, lax.axis_size("z"))], axis=0)
    return jnp.concatenate([x, swap(x, "c")], axis=0)


def gather_blocks(block):
    parts = [part[None, None] for part in jnp.split(block, len(PATHS), axis=0)]
    for step in range(len(PATHS[0])):
        for q, path in enumerate(PATHS):
            axis, mask = path[step]
            place = ("x", "y").index(axis)
            index = lax.axis_index(axis)
            own, other = parts[q], swap(parts[q], axis, mask)
            second = (axis, 4 - mask) in path[:step]
            if mask == 3:
                first = index < 2
            elif second:
                first = (index == 0) | (index == 3)
            else:
                first = index % 2 == 0
            lower, upper = jnp.where(first, own, other), jnp.where(first, other, own)
            if second and mask == 1:
                lower, upper = jnp.split(lower, 2, axis=place), jnp.split(upper, 2, axis=place)
                pieces = [lower[0], upper[0], upper[1], lower[1]]
            else:
                pieces = [lower, upper]
            parts[q] = jnp.concatenate(pieces, axis=place)
    parts = [part.reshape((-1,) + part.shape[2:]) for part in parts]
    return jnp.concatenate(parts, axis=1)


def slope(gradient, packed, width):
    unit = packed[:, :width].astype(jnp.float32)
    length = jnp.sum(packed[:, width:].astype(jnp.float32), axis=1, keepdims=True)
    along = jnp.sum(unit * gradient, axis=1, keepdims=True)
    return ((gradient - unit * along) / length).astype(jnp.bfloat16)


def per_device(image_x, text_x, image_gain, text_gain, image_w, text_w, sharpness, offset):
    scale, bias = sharpness[0], offset[0]
    towers = lax.axis_size("t")
    rows, width = image_x.shape[0], image_w.shape[1]
    image_values = image_x.astype(jnp.float32)
    text_values = text_x.astype(jnp.float32)
    moments = lax.psum(
        (
            jnp.sum(image_values, axis=1),
            jnp.sum(image_values * image_values, axis=1),
            jnp.sum(text_values, axis=1),
            jnp.sum(text_values * text_values, axis=1),
        ),
        "t",
    )
    image_normed = normed_half(
        image_values, moments[0], moments[1], image_x.shape[1] * towers, image_gain
    )
    text_normed = normed_half(
        text_values, moments[2], moments[3], text_x.shape[1] * towers, text_gain
    )
    image_part = jnp.dot(image_normed, image_w, preferred_element_type=jnp.float32)
    text_part = jnp.dot(text_normed, text_w, preferred_element_type=jnp.float32)
    image_pre = image_part + swap(image_part.astype(jnp.bfloat16), "t").astype(jnp.float32)
    text_pre = text_part + swap(text_part.astype(jnp.bfloat16), "t").astype(jnp.float32)
    image_rows = gather_xy(packed_rows(image_pre))
    text_rows = gather_zc(packed_rows(text_pre))
    image_normed_rows = gather_xy(image_normed)
    text_normed_rows = gather_zc(text_normed)

    image_units, text_units = image_rows[:, :width], text_rows[:, :width]
    products = lax.dot_general(
        image_units, text_units, (((1,), (1,)), ((), ())), preferred_element_type=jnp.float32
    )
    logits = scale * products + bias
    sizes = {axis: lax.axis_size(axis) for axis in DP}
    quarter, chips = rows // len(PATHS), sizes["x"] * sizes["y"]
    row_ids = lax.broadcasted_iota(jnp.int32, products.shape, 0)
    inner = row_ids % (quarter * chips)
    row_ids = (row_ids // (quarter * chips)) * quarter + inner
    column_ids = lax.broadcasted_iota(jnp.int32, products.shape, 1)
    same = (row_ids == column_ids) & (inner < quarter)
    labels = jnp.where(same, 1.0, -1.0).astype(jnp.float32)
    weights = (-labels * jax.nn.sigmoid(-labels * logits)).astype(jnp.bfloat16)
    image_grad = scale * jnp.dot(weights, text_units, preferred_element_type=jnp.float32)
    text_grad = scale * lax.dot_general(
        weights, image_units, (((0,), (0,)), ((), ())), preferred_element_type=jnp.float32
    )
    image_slope = slope(image_grad, image_rows, width)
    text_slope = slope(text_grad, text_rows, width)
    image_term = lax.dot_general(
        image_normed_rows, image_slope, (((0,), (0,)), ((), ())), preferred_element_type=jnp.float32
    )
    text_term = lax.dot_general(
        text_normed_rows, text_slope, (((0,), (0,)), ((), ())), preferred_element_type=jnp.float32
    )
    term = jnp.concatenate([image_term, text_term], axis=0)
    half = width // 2
    first = lax.axis_index("c") == 0
    kept = jnp.where(first, term[:, :half], term[:, half:])
    sent = jnp.where(first, term[:, half:], term[:, :half])
    kept = (kept + swap(sent, "c")).astype(jnp.bfloat16)
    deep = kept.shape[0]
    each = -(-deep // (chips * 32)) * 32
    kept = jnp.pad(kept, ((0, chips * each - deep), (0, 0)))
    blocks = lax.all_to_all(kept.reshape(chips, each, half), ("x", "y"), 0, 0)
    block = jnp.sum(blocks.astype(jnp.float32), axis=0).astype(jnp.bfloat16)
    others = [swap(block, "z", k).astype(jnp.float32) for k in range(1, sizes["z"])]
    block = (block.astype(jnp.float32) + others[0]) + (others[1] + others[2])
    block = gather_blocks(block.astype(jnp.bfloat16)).reshape(chips * each, half)[:deep]
    other = swap(block, "c")
    full = jnp.concatenate(
        [jnp.where(first, block, other), jnp.where(first, other, block)], axis=1
    ).astype(jnp.float32)
    depth = image_w.shape[0]
    return full[:depth], full[depth:]


def solution(mesh):
    grid = Mesh(mesh.devices.reshape(2, 4, 4, 4, 2), AXES)
    return jax.shard_map(
        per_device,
        mesh=grid,
        in_specs=(
            P(DP, "t"),
            P(DP, "t"),
            P("t"),
            P("t"),
            P("t", None),
            P("t", None),
            P(),
            P(),
        ),
        out_specs=(P("t", None), P("t", None)),
        check_vma=False,
    )
```

```python
import jax
import jax.numpy as jnp
from jax import lax
from jax.sharding import Mesh, PartitionSpec as P

AXES = ("t", "z", "x", "y", "c")
DP = ("z", "x", "y", "c")


def swap(x, axis, mask=1):
    return lax.ppermute(x, axis, [(i, i ^ mask) for i in range(lax.axis_size(axis))])


def normed_half(values, sums, squares, width, gain):
    average = (sums / width)[:, None]
    inverse = lax.rsqrt((squares / width)[:, None] - average * average + 1e-06)
    return ((values - average) * inverse * gain[None, :]).astype(jnp.bfloat16)


def split3(x):
    high = x.astype(jnp.bfloat16)
    rest = x - high.astype(jnp.float32)
    mid = rest.astype(jnp.bfloat16)
    low = (rest - mid.astype(jnp.float32)).astype(jnp.bfloat16)
    column = lax.broadcasted_iota(jnp.int32, (x.shape[0], 128), 1)
    zero = jnp.zeros((), jnp.bfloat16)
    return jnp.where(
        column == 0, high, jnp.where(column == 1, mid, jnp.where(column == 2, low, zero))
    )


def packed_rows(projected):
    length = jnp.sqrt(jnp.sum(projected * projected, axis=1, keepdims=True) + 1e-06)
    unit = (projected / length).astype(jnp.bfloat16)
    return jnp.concatenate([unit, split3(length)], axis=1)


def ordered(own, other, axis, mask, second, place):
    index = lax.axis_index(axis)
    if mask == 3:
        first = index < 2
    elif second:
        first = (index == 0) | (index == 3)
    else:
        first = index % 2 == 0
    lower, upper = jnp.where(first, own, other), jnp.where(first, other, own)
    if second and mask == 1:
        lower, upper = jnp.split(lower, 2, axis=place), jnp.split(upper, 2, axis=place)
        pieces = [lower[0], upper[0], upper[1], lower[1]]
    else:
        pieces = [lower, upper]
    return jnp.concatenate(pieces, axis=place)


def gather_xy(block):
    parts = [part[None, None] for part in jnp.split(block, 2, axis=0)]
    for phase in range(2):
        axes = ("x", "y") if phase == 0 else ("x", "x", "y", "y")
        masks = ((1, 1), (3, 3)) if phase == 0 else ((1, 3, 1, 3), (3, 1, 3, 1))
        if phase == 1:
            parts = [half for part in parts[::-1] for half in jnp.split(part, 2, axis=2)]
        for step in range(2):
            others = [swap(p, a, m) for p, a, m in zip(parts, axes, masks[step])]
            others = lax.optimization_barrier(others)
            parts = [
                ordered(p, o, a, m, step == 1, ("x", "y").index(a))
                for p, o, a, m in zip(parts, others, axes, masks[step])
            ]
    parts = [part.reshape((-1,) + part.shape[2:]) for part in parts]
    return jnp.concatenate(parts[2:] + parts[:2], axis=1)


def by_core(x):
    other = swap(x, "c")
    first = lax.axis_index("c") == 0
    return jnp.concatenate([jnp.where(first, x, other), jnp.where(first, other, x)], axis=0)


def gather_zc(x):
    parts = [x] + [swap(x, "z", k) for k in range(1, lax.axis_size("z"))]
    parts = [parts[0]] + list(lax.optimization_barrier(parts[1:]))
    index = lax.axis_index("z")
    even, low = index % 2 == 0, index < 2
    pairs = [
        [jnp.where(even, a, b), jnp.where(even, b, a)] for a, b in (parts[:2], parts[2:])
    ]
    parts = [jnp.where(low, a, b) for a, b in zip(*pairs)] + [
        jnp.where(low, b, a) for a, b in zip(*pairs)
    ]
    return by_core(jnp.concatenate(parts, axis=0))


def slope(gradient, packed, width):
    unit = packed[:, :width].astype(jnp.float32)
    length = jnp.sum(packed[:, width:].astype(jnp.float32), axis=1, keepdims=True)
    along = jnp.sum(unit * gradient, axis=1, keepdims=True)
    return ((gradient - unit * along) / length).astype(jnp.bfloat16)


def per_device(image_x, text_x, image_gain, text_gain, image_w, text_w, sharpness, offset):
    scale, bias = sharpness[0], offset[0]
    towers = lax.axis_size("t")
    rows, width = image_x.shape[0], image_w.shape[1]
    image_values = image_x.astype(jnp.float32)
    text_values = text_x.astype(jnp.float32)
    moments = lax.psum(
        (
            jnp.sum(image_values, axis=1),
            jnp.sum(image_values * image_values, axis=1),
            jnp.sum(text_values, axis=1),
            jnp.sum(text_values * text_values, axis=1),
        ),
        "t",
    )
    image_normed = normed_half(
        image_values, moments[0], moments[1], image_x.shape[1] * towers, image_gain
    )
    text_normed = normed_half(
        text_values, moments[2], moments[3], text_x.shape[1] * towers, text_gain
    )
    image_part = jnp.dot(image_normed, image_w, preferred_element_type=jnp.float32)
    text_part = jnp.dot(text_normed, text_w, preferred_element_type=jnp.float32)
    image_pre = image_part + swap(image_part.astype(jnp.bfloat16), "t").astype(jnp.float32)
    text_pre = text_part + swap(text_part.astype(jnp.bfloat16), "t").astype(jnp.float32)
    text_rows = gather_xy(packed_rows(text_pre)).reshape(-1, width + 128)
    image_rows = gather_zc(packed_rows(image_pre))
    text_normed_rows = lax.all_gather(text_normed, "y", axis=0, tiled=True)
    text_normed_rows = lax.all_gather(text_normed_rows, "x", axis=0, tiled=True)
    image_normed_rows = by_core(lax.all_gather(image_normed, "z", axis=0, tiled=True))

    image_units, text_units = image_rows[:, :width], text_rows[:, :width]
    products = lax.dot_general(
        image_units, text_units, (((1,), (1,)), ((), ())), preferred_element_type=jnp.float32
    )
    logits = scale * products + bias
    sizes = {axis: lax.axis_size(axis) for axis in DP}
    own_image = (lax.axis_index("c") * sizes["z"] + lax.axis_index("z")) * rows
    own_text = (lax.axis_index("x") * sizes["y"] + lax.axis_index("y")) * rows
    row_ids = lax.broadcasted_iota(jnp.int32, products.shape, 0) - own_image
    column_ids = lax.broadcasted_iota(jnp.int32, products.shape, 1) - own_text
    same = (row_ids == column_ids) & (row_ids >= 0) & (row_ids < rows)
    labels = jnp.where(same, 1.0, -1.0).astype(jnp.float32)
    weights = (-labels * jax.nn.sigmoid(-labels * logits)).astype(jnp.bfloat16)
    image_grad = scale * jnp.dot(weights, text_units, preferred_element_type=jnp.float32)
    text_grad = scale * lax.dot_general(
        weights, image_units, (((0,), (0,)), ((), ())), preferred_element_type=jnp.float32
    )
    image_slope = slope(image_grad, image_rows, width)
    text_slope = slope(text_grad, text_rows, width)
    image_term = lax.dot_general(
        image_normed_rows, image_slope, (((0,), (0,)), ((), ())), preferred_element_type=jnp.float32
    )
    text_term = lax.dot_general(
        text_normed_rows, text_slope, (((0,), (0,)), ((), ())), preferred_element_type=jnp.float32
    )
    term = jnp.concatenate([image_term, text_term], axis=0)
    half = width // 2
    first = lax.axis_index("c") == 0
    kept = jnp.where(first, term[:, :half], term[:, half:])
    sent = jnp.where(first, term[:, half:], term[:, :half])
    kept = (kept + swap(sent, "c")).astype(jnp.bfloat16)
    deep = kept.shape[0]
    chips = sizes["x"] * sizes["y"]
    each = -(-deep // (chips * 32)) * 32
    kept = jnp.pad(kept, ((0, chips * each - deep), (0, 0)))
    blocks = lax.all_to_all(kept.reshape(chips, each, half), ("x", "y"), 0, 0)
    block = jnp.sum(blocks.astype(jnp.float32), axis=0).astype(jnp.bfloat16)
    others = [swap(block, "z", k).astype(jnp.float32) for k in range(1, sizes["z"])]
    block = (block.astype(jnp.float32) + others[0]) + (others[1] + others[2])
    block = gather_xy(block.astype(jnp.bfloat16)).reshape(chips * each, half)[:deep]
    other = swap(block, "c")
    full = jnp.concatenate(
        [jnp.where(first, block, other), jnp.where(first, other, block)], axis=1
    ).astype(jnp.float32)
    depth = image_w.shape[0]
    return full[:depth], full[depth:]


def solution(mesh):
    grid = Mesh(mesh.devices.reshape(2, 4, 4, 4, 2), AXES)
    return jax.shard_map(
        per_device,
        mesh=grid,
        in_specs=(
            P(DP, "t"),
            P(DP, "t"),
            P("t"),
            P("t"),
            P("t", None),
            P("t", None),
            P(),
            P(),
        ),
        out_specs=(P("t", None), P("t", None)),
        check_vma=False,
    )
```

```python
import jax
import jax.numpy as jnp
from jax import lax
from jax.sharding import Mesh, PartitionSpec as P

AXES = ("t", "z", "x", "y", "c")
DP = ("z", "x", "y", "c")


def swap(x, axis, mask=1):
    return lax.ppermute(x, axis, [(i, i ^ mask) for i in range(lax.axis_size(axis))])


def row_scales(sums, squares, width):
    average = sums / width
    return average, lax.rsqrt(squares / width - average * average + 1e-06)


def normed(values, average, inverse, gain):
    values = values.astype(jnp.float32)
    return ((values - average) * inverse * gain[None, :]).astype(jnp.bfloat16)


def rounded(x):
    return lax.reduce_precision(x, 8, 7)


def columns_of(vectors, count=128):
    column = lax.broadcasted_iota(jnp.int32, (vectors[0].shape[0], count), 1)
    block = jnp.zeros(column.shape, jnp.float32)
    for i, rest in enumerate(vectors):
        for k in range(3):
            piece = rounded(rest)
            block = jnp.where(column == 3 * i + k, piece[:, None], block)
            rest = rest - piece
    return block.astype(jnp.bfloat16)


def vector_of(block, i):
    return jnp.sum(block[:, 3 * i : 3 * i + 3].astype(jnp.float32), axis=1, keepdims=True)


def packed_rows(projected, average, inverse):
    length = jnp.sqrt(jnp.sum(projected * projected, axis=1, keepdims=True) + 1e-06)
    unit = (projected / length).astype(jnp.bfloat16)
    return jnp.concatenate([unit, columns_of([length[:, 0], average, inverse])], axis=1)


def tied(*arrays):
    return lax.optimization_barrier(arrays)


def gather_text(x):
    halves = jnp.split(x, 2, axis=0)
    orders = ((("x", 1), ("x", 3), ("y", 1)), (("y", 1), ("x", 1), ("x", 3)))
    for step in range(3):
        others = tied(*[swap(h, *order[step]) for h, order in zip(halves, orders)])
        halves = [jnp.concatenate([h, o], axis=0) for h, o in zip(halves, others)]
    return both_cores(jnp.concatenate(halves, axis=0))


def gather_image(x):
    first = swap(x, "y", 3)
    along = jnp.concatenate(tied(*[swap(x, "z", k) for k in (2, 3, 1)]), axis=0)
    return jnp.concatenate([x, along, first, swap(along, "y", 3)], axis=0)


def both_cores(x):
    return jnp.concatenate([x, swap(x, "c")], axis=0)


def by_index(parts, axis):
    index = lax.axis_index(axis)
    even, low = index % 2 == 0, index < 2
    pairs = [
        [jnp.where(even, a, b), jnp.where(even, b, a)] for a, b in (parts[:2], parts[2:])
    ]
    return [jnp.where(low, a, b) for a, b in zip(*pairs)] + [
        jnp.where(low, b, a) for a, b in zip(*pairs)
    ]


def gather_xy(block):
    parts = [part[None, None] for part in jnp.split(block, 2, axis=0)]
    for axes in (("x", "y"), ("y", "x")):
        others = tied(
            *[swap(part, axis, k) for k in (2, 1, 3) for part, axis in zip(parts, axes)]
        )
        parts = [
            jnp.concatenate(
                by_index([part, others[2 + i], others[i], others[4 + i]], axis),
                axis=("x", "y").index(axis),
            )
            for i, (part, axis) in enumerate(zip(parts, axes))
        ]
    parts = [part.reshape((-1,) + part.shape[2:]) for part in parts]
    return jnp.concatenate(parts, axis=1)


def slope(gradient, packed, width):
    unit = packed[:, :width].astype(jnp.float32)
    length = vector_of(packed[:, width:], 0)
    along = jnp.sum(unit * gradient, axis=1, keepdims=True)
    value = (gradient - unit * along) / length
    high = rounded(value)
    return high.astype(jnp.bfloat16), (value - high).astype(jnp.bfloat16)


def over_rows(features, slopes):
    return sum(
        lax.dot_general(
            features, part, (((0,), (0,)), ((), ())), preferred_element_type=jnp.float32
        )
        for part in slopes
    )


def per_device(image_x, text_x, image_gain, text_gain, image_w, text_w, sharpness, offset):
    scale, bias = sharpness[0], offset[0]
    towers = lax.axis_size("t")
    rows, width = image_x.shape[0], image_w.shape[1]
    image_values = image_x.astype(jnp.float32)
    text_values = text_x.astype(jnp.float32)
    text_1, image_y = swap(text_x, "x", 1), swap(image_x, "y", 3)
    image_z = [swap(image_x, "z", k) for k in (2, 3, 1)]
    moments = lax.psum(
        (
            jnp.sum(image_values, axis=1),
            jnp.sum(image_values * image_values, axis=1),
            jnp.sum(text_values, axis=1),
            jnp.sum(text_values * text_values, axis=1),
        ),
        "t",
    )
    moments, text_1, image_y, image_z = tied(moments, text_1, image_y, image_z)
    image_scales = row_scales(moments[0], moments[1], image_x.shape[1] * towers)
    text_scales = row_scales(moments[2], moments[3], text_x.shape[1] * towers)
    image_part = jnp.dot(
        normed(image_x, *[v[:, None] for v in image_scales], image_gain),
        image_w,
        preferred_element_type=jnp.float32,
    )
    text_part = jnp.dot(
        normed(text_x, *[v[:, None] for v in text_scales], text_gain),
        text_w,
        preferred_element_type=jnp.float32,
    )
    text_2, image_z = jnp.concatenate([text_x, text_1], axis=0), jnp.concatenate(image_z, axis=0)
    image_far = swap(image_z, "y", 3)
    image_send, text_send, text_3 = tied(
        image_part, text_part, swap(text_2, "x", 3)
    )
    image_other, text_other = swap(image_send, "t"), swap(text_send, "t")
    text_4 = jnp.concatenate([text_2, text_3], axis=0)
    text_8 = jnp.concatenate([text_4, swap(text_4, "y", 1)], axis=0)
    text_other, image_other, text_8, image_far = tied(text_other, image_other, text_8, image_far)
    text_rows = gather_text(packed_rows(text_send + text_other, *text_scales))
    image_rows = gather_image(
        packed_rows(image_send + image_other, *image_scales)
    )
    image_features = jnp.concatenate([image_x, image_z, image_y, image_far], axis=0)
    chips = text_8.reshape(2, 2, 2, 2, rows // 2, text_x.shape[1])
    text_features = both_cores(
        jnp.concatenate(
            [
                chips[:, :, :, 0].reshape(-1, text_x.shape[1]),
                chips[:, :, :, 1].transpose(1, 2, 0, 3, 4).reshape(-1, text_x.shape[1]),
            ],
            axis=0,
        )
    )
    image_normed_rows, text_normed_rows = (
        normed(features, vector_of(block, 1), vector_of(block, 2), gain)
        for features, block, gain in (
            (image_features, image_rows[:, width:], image_gain),
            (text_features, text_rows[:, width:], text_gain),
        )
    )

    image_units, text_units = image_rows[:, :width], text_rows[:, :width]
    products = lax.dot_general(
        image_units, text_units, (((1,), (1,)), ((), ())), preferred_element_type=jnp.float32
    )
    logits = scale * products + bias
    half = rows // 2
    row_ids = lax.broadcasted_iota(jnp.int32, products.shape, 0)
    column_ids = lax.broadcasted_iota(jnp.int32, products.shape, 1)
    same = ((column_ids == row_ids) & (row_ids < half)) | (
        (column_ids == row_ids + 7 * half) & (row_ids >= half) & (row_ids < rows)
    )
    labels = jnp.where(same, 1.0, -1.0).astype(jnp.float32)
    weights = (-labels * jax.nn.sigmoid(-labels * logits)).astype(jnp.bfloat16)
    image_grad = scale * jnp.dot(weights, text_units, preferred_element_type=jnp.float32)
    text_grad = scale * lax.dot_general(
        weights, image_units, (((0,), (0,)), ((), ())), preferred_element_type=jnp.float32
    )
    image_slope = slope(image_grad, image_rows, width)
    text_slope = slope(text_grad, text_rows, width)
    image_term = over_rows(image_normed_rows, image_slope)
    text_term = over_rows(text_normed_rows, text_slope)
    plane = lax.axis_size("x") * lax.axis_size("y")
    deep, depth = image_w.shape[0] + text_w.shape[0], image_w.shape[0]
    each = -(-deep // (2 * plane * 16)) * 16
    term = jnp.concatenate(
        [image_term, text_term, jnp.zeros((2 * plane * each - deep, width), jnp.float32)], axis=0
    )
    lower, upper = jnp.split(term, 2, axis=0)
    first = lax.axis_index("c") == 0
    kept = jnp.where(first, lower, upper) + swap(jnp.where(first, upper, lower), "c")
    blocks = kept.astype(jnp.bfloat16).reshape(plane, each, width)
    blocks = lax.all_to_all(blocks, ("x", "y"), 0, 0)
    block = rounded(jnp.sum(blocks.astype(jnp.float32), axis=0))
    others = tied(*[swap(block.astype(jnp.bfloat16), "z", k) for k in (2, 3, 1)])
    z2, z3, z1 = [other.astype(jnp.float32) for other in others]
    block = ((block + z1) + (z2 + z3)).astype(jnp.bfloat16)
    block = gather_xy(block).reshape(plane * each, width)
    other = swap(block, "c")
    full = jnp.concatenate(
        [jnp.where(first, block, other), jnp.where(first, other, block)], axis=0
    ).astype(jnp.float32)
    return full[:depth], full[depth:deep]


def solution(mesh):
    grid = Mesh(mesh.devices.reshape(2, 4, 4, 4, 2), AXES)
    return jax.shard_map(
        per_device,
        mesh=grid,
        in_specs=(
            P(DP, "t"),
            P(DP, "t"),
            P("t"),
            P("t"),
            P("t", None),
            P("t", None),
            P(),
            P(),
        ),
        out_specs=(P("t", None), P("t", None)),
        check_vma=False,
    )
```

```python
import jax
import jax.numpy as jnp
from jax import lax
from jax.sharding import Mesh, PartitionSpec as P

AXES = ("t", "z", "x", "y", "c")
DP = ("z", "x", "y", "c")


def swap(x, axis, mask=1):
    return lax.ppermute(x, axis, [(i, i ^ mask) for i in range(lax.axis_size(axis))])


def row_scales(sums, squares, width):
    average = sums / width
    return average, lax.rsqrt(squares / width - average * average + 1e-06)


def normed(values, average, inverse, gain):
    values = values.astype(jnp.float32)
    return ((values - average) * inverse * gain[None, :]).astype(jnp.bfloat16)


def rounded(x):
    return lax.reduce_precision(x, 8, 7)


def columns_of(vectors, count=128):
    column = lax.broadcasted_iota(jnp.int32, (vectors[0].shape[0], count), 1)
    block = jnp.zeros(column.shape, jnp.float32)
    for i, rest in enumerate(vectors):
        for k in range(3):
            piece = rounded(rest)
            block = jnp.where(column == 3 * i + k, piece[:, None], block)
            rest = rest - piece
    return block.astype(jnp.bfloat16)


def vector_of(block, i):
    return jnp.sum(block[:, 3 * i : 3 * i + 3].astype(jnp.float32), axis=1, keepdims=True)


def unit_scaled(part):
    norm = jnp.sqrt(jnp.mean(part * part, axis=1) + 1e-30)
    return (part / norm[:, None]).astype(jnp.float16), norm


def packed_rows(projected, average, inverse):
    length = jnp.sqrt(jnp.sum(projected * projected, axis=1, keepdims=True) + 1e-06)
    unit = (projected / length).astype(jnp.bfloat16)
    return jnp.concatenate([unit, columns_of([length[:, 0], average, inverse])], axis=1)


def tied(*arrays):
    return lax.optimization_barrier(arrays)


def gather_rows(text, image):
    low, high = jnp.split(text, 2, axis=0)
    image_z = [swap(image, "z", k) for k in (2, 3, 1)]
    low_1, high_1 = tied(swap(low, "x", 1), swap(high, "y", 1))
    low, high = jnp.concatenate([low, low_1], axis=0), jnp.concatenate([high, high_1], axis=0)
    image_y = swap(image, "y", 3)
    low_1, high_1, *image_z = tied(swap(low, "x", 3), swap(high, "x", 1), *image_z)
    image_z = jnp.concatenate(image_z, axis=0)
    low, high = jnp.concatenate([low, low_1], axis=0), jnp.concatenate([high, high_1], axis=0)
    image_far = swap(image_z, "y", 3)
    low_1, high_1 = swap(low, "y", 1), swap(high, "x", 3)
    text = both_cores(jnp.concatenate([low, low_1, high, high_1], axis=0))
    return text, jnp.concatenate([image, image_z, image_y, image_far], axis=0)


def both_cores(x):
    return jnp.concatenate([x, swap(x, "c")], axis=0)


def by_index(parts, axis):
    index = lax.axis_index(axis)
    even, low = index % 2 == 0, index < 2
    pairs = [
        [jnp.where(even, a, b), jnp.where(even, b, a)] for a, b in (parts[:2], parts[2:])
    ]
    return [jnp.where(low, a, b) for a, b in zip(*pairs)] + [
        jnp.where(low, b, a) for a, b in zip(*pairs)
    ]


def gather_xy(block):
    parts = [part[None, None] for part in jnp.split(block, 2, axis=0)]
    for axes in (("x", "y"), ("y", "x")):
        others = tied(
            *[swap(part, axis, k) for k in (2, 1, 3) for part, axis in zip(parts, axes)]
        )
        parts = [
            jnp.concatenate(
                by_index([part, others[2 + i], others[i], others[4 + i]], axis),
                axis=("x", "y").index(axis),
            )
            for i, (part, axis) in enumerate(zip(parts, axes))
        ]
    parts = [part.reshape((-1,) + part.shape[2:]) for part in parts]
    return jnp.concatenate(parts, axis=1)


def slope(gradient, packed, width):
    unit = packed[:, :width].astype(jnp.float32)
    length = vector_of(packed[:, width:], 0)
    along = jnp.sum(unit * gradient, axis=1, keepdims=True)
    value = (gradient - unit * along) / length
    high = rounded(value)
    return high.astype(jnp.bfloat16), (value - high).astype(jnp.bfloat16)


def over_rows(features, slopes):
    return sum(
        lax.dot_general(
            features, part, (((0,), (0,)), ((), ())), preferred_element_type=jnp.float32
        )
        for part in slopes
    )


def per_device(image_x, text_x, image_gain, text_gain, image_w, text_w, sharpness, offset):
    scale, bias = sharpness[0], offset[0]
    towers = lax.axis_size("t")
    rows, width = image_x.shape[0], image_w.shape[1]
    image_values = image_x.astype(jnp.float32)
    text_values = text_x.astype(jnp.float32)
    moments = jnp.stack(
        [
            jnp.sum(image_values, axis=1),
            jnp.sum(image_values * image_values, axis=1),
            jnp.sum(text_values, axis=1),
            jnp.sum(text_values * text_values, axis=1),
        ]
    )
    moments, text_0, image_0 = tied(moments, text_x, image_x)
    moments_1 = swap(moments, "t")
    text_1, image_y = swap(text_0, "x", 1), swap(image_0, "y", 3)
    image_z = [swap(image_0, "z", k) for k in (2, 3, 1)]
    moments_1, text_1, image_y, image_z = tied(moments_1, text_1, image_y, image_z)
    moments = moments + moments_1
    image_scales = row_scales(moments[0], moments[1], image_x.shape[1] * towers)
    text_scales = row_scales(moments[2], moments[3], text_x.shape[1] * towers)
    image_part = jnp.dot(
        normed(image_x, *[v[:, None] for v in image_scales], image_gain),
        image_w,
        preferred_element_type=jnp.float32,
    )
    text_part = jnp.dot(
        normed(text_x, *[v[:, None] for v in text_scales], text_gain),
        text_w,
        preferred_element_type=jnp.float32,
    )
    text_2, image_z = jnp.concatenate([text_x, text_1], axis=0), jnp.concatenate(image_z, axis=0)
    image_far = swap(image_z, "y", 3)
    image_send, image_norm = unit_scaled(image_part)
    text_send, text_norm = unit_scaled(text_part)
    norms, image_send, text_send, text_3 = tied(
        jnp.stack([image_norm, text_norm]), image_send, text_send, swap(text_2, "x", 3)
    )
    image_other, text_other = swap(image_send, "t"), swap(text_send, "t")
    norms = swap(norms, "t")
    text_4 = jnp.concatenate([text_2, text_3], axis=0)
    text_8 = jnp.concatenate([text_4, swap(text_4, "y", 1)], axis=0)
    norms, text_other, image_other, text_8, image_far = tied(
        norms, text_other, image_other, text_8, image_far
    )
    image_pre = image_part + image_other.astype(jnp.float32) * norms[0][:, None]
    text_pre = text_part + text_other.astype(jnp.float32) * norms[1][:, None]
    text_rows, image_rows = gather_rows(
        packed_rows(text_pre, *text_scales), packed_rows(image_pre, *image_scales)
    )
    image_features = jnp.concatenate([image_x, image_z, image_y, image_far], axis=0)
    chips = text_8.reshape(2, 2, 2, 2, rows // 2, text_x.shape[1])
    text_features = both_cores(
        jnp.concatenate(
            [
                chips[:, :, :, 0].reshape(-1, text_x.shape[1]),
                chips[:, :, :, 1].transpose(1, 2, 0, 3, 4).reshape(-1, text_x.shape[1]),
            ],
            axis=0,
        )
    )
    image_normed_rows, text_normed_rows = (
        normed(features, vector_of(block, 1), vector_of(block, 2), gain)
        for features, block, gain in (
            (image_features, image_rows[:, width:], image_gain),
            (text_features, text_rows[:, width:], text_gain),
        )
    )

    image_units, text_units = image_rows[:, :width], text_rows[:, :width]
    products = lax.dot_general(
        image_units, text_units, (((1,), (1,)), ((), ())), preferred_element_type=jnp.float32
    )
    logits = scale * products + bias
    half = rows // 2
    row_ids = lax.broadcasted_iota(jnp.int32, products.shape, 0)
    column_ids = lax.broadcasted_iota(jnp.int32, products.shape, 1)
    same = ((column_ids == row_ids) & (row_ids < half)) | (
        (column_ids == row_ids + 7 * half) & (row_ids >= half) & (row_ids < rows)
    )
    labels = jnp.where(same, 1.0, -1.0).astype(jnp.float32)
    weights = (-labels * jax.nn.sigmoid(-labels * logits)).astype(jnp.bfloat16)
    image_grad = scale * jnp.dot(weights, text_units, preferred_element_type=jnp.float32)
    text_grad = scale * lax.dot_general(
        weights, image_units, (((0,), (0,)), ((), ())), preferred_element_type=jnp.float32
    )
    image_slope = slope(image_grad, image_rows, width)
    text_slope = slope(text_grad, text_rows, width)
    image_term = over_rows(image_normed_rows, image_slope)
    text_term = over_rows(text_normed_rows, text_slope)
    plane = lax.axis_size("x") * lax.axis_size("y")
    deep, depth = image_w.shape[0] + text_w.shape[0], image_w.shape[0]
    each = -(-deep // (2 * plane * 16)) * 16
    term = jnp.concatenate(
        [image_term, text_term, jnp.zeros((2 * plane * each - deep, width), jnp.float32)], axis=0
    )
    lower, upper = jnp.split(term, 2, axis=0)
    first = lax.axis_index("c") == 0
    kept = jnp.where(first, lower, upper) + swap(jnp.where(first, upper, lower), "c")
    blocks = kept.astype(jnp.bfloat16).reshape(plane, each, width)
    blocks = lax.all_to_all(blocks, ("x", "y"), 0, 0)
    block = rounded(jnp.sum(blocks.astype(jnp.float32), axis=0))
    others = tied(*[swap(block.astype(jnp.bfloat16), "z", k) for k in (2, 3, 1)])
    z2, z3, z1 = [other.astype(jnp.float32) for other in others]
    block = ((block + z1) + (z2 + z3)).astype(jnp.bfloat16)
    block = gather_xy(block).reshape(plane * each, width)
    other = swap(block, "c")
    lower, upper = jnp.where(first, block, other), jnp.where(first, other, block)
    split = depth - plane * each
    return (
        jnp.concatenate([lower, upper[:split]], axis=0).astype(jnp.float32),
        upper[split : deep - plane * each].astype(jnp.float32),
    )


def solution(mesh):
    grid = Mesh(mesh.devices.reshape(2, 4, 4, 4, 2), AXES)
    return jax.shard_map(
        per_device,
        mesh=grid,
        in_specs=(
            P(DP, "t"),
            P(DP, "t"),
            P("t"),
            P("t"),
            P("t", None),
            P("t", None),
            P(),
            P(),
        ),
        out_specs=(P("t", None), P("t", None)),
        check_vma=False,
    )
```

```python
import jax
import jax.numpy as jnp
from jax import lax
from jax.sharding import Mesh, PartitionSpec as P

AXES = ("t", "z", "x", "y", "c")
DP = ("z", "x", "y", "c")


def swap(x, axis, mask=1):
    return lax.ppermute(x, axis, [(i, i ^ mask) for i in range(lax.axis_size(axis))])


def row_scales(sums, squares, width):
    average = sums / width
    return average, lax.rsqrt(squares / width - average * average + 1e-06)


def normed(values, average, inverse, gain):
    values = values.astype(jnp.float32)
    return ((values - average) * inverse * gain[None, :]).astype(jnp.bfloat16)


def rounded(x):
    return lax.reduce_precision(x, 8, 7)


def columns_of(vectors, count=128):
    column = lax.broadcasted_iota(jnp.int32, (vectors[0].shape[0], count), 1)
    block = jnp.zeros(column.shape, jnp.float32)
    for i, rest in enumerate(vectors):
        for k in range(3):
            piece = rounded(rest)
            block = jnp.where(column == 3 * i + k, piece[:, None], block)
            rest = rest - piece
    return block.astype(jnp.bfloat16)


def vector_of(block, i):
    return jnp.sum(block[:, 3 * i : 3 * i + 3].astype(jnp.float32), axis=1, keepdims=True)


def unit_scaled(part):
    norm = jnp.sqrt(jnp.mean(part * part, axis=1) + 1e-30)
    return (part / norm[:, None]).astype(jnp.float16), norm


def packed_rows(projected, average, inverse):
    length = jnp.sqrt(jnp.sum(projected * projected, axis=1, keepdims=True) + 1e-06)
    unit = (projected / length).astype(jnp.bfloat16)
    return jnp.concatenate([unit, columns_of([length[:, 0], average, inverse])], axis=1)


def tied(*arrays):
    return lax.optimization_barrier(arrays)


def gather_rows(text, image):
    low, high = jnp.split(text, 2, axis=0)
    image_z = [swap(image, "z", k) for k in (1, 2, 3)]
    low_1, high_1, near = tied(swap(low, "x", 1), swap(high, "y", 1), image_z[0])
    image_y = [swap(image, "y", 3), swap(near, "y", 3)]
    low, high = jnp.concatenate([low, low_1], axis=0), jnp.concatenate([high, high_1], axis=0)
    low_1, high_1, *image_z = tied(swap(low, "x", 3), swap(high, "x", 1), *image_z[1:])
    far = jnp.concatenate(image_z, axis=0)
    low, high = jnp.concatenate([low, low_1], axis=0), jnp.concatenate([high, high_1], axis=0)
    low_1, high_1, *image_y = tied(swap(low, "y", 1), swap(high, "x", 3), *image_y, swap(far, "y", 3))
    text = both_cores(jnp.concatenate([low, low_1, high, high_1], axis=0))
    return text, jnp.concatenate([image, near, far] + image_y, axis=0)


def both_cores(x):
    return jnp.concatenate([x, swap(x, "c")], axis=0)


def by_index(parts, axis):
    index = lax.axis_index(axis)
    even, low = index % 2 == 0, index < 2
    pairs = [
        [jnp.where(even, a, b), jnp.where(even, b, a)] for a, b in (parts[:2], parts[2:])
    ]
    return [jnp.where(low, a, b) for a, b in zip(*pairs)] + [
        jnp.where(low, b, a) for a, b in zip(*pairs)
    ]


def gather_xy(block):
    parts = [part[None, None] for part in jnp.split(block, 2, axis=0)]
    for axes in (("x", "y"), ("y", "x")):
        others = tied(
            *[swap(part, axis, k) for k in (2, 1, 3) for part, axis in zip(parts, axes)]
        )
        parts = [
            jnp.concatenate(
                by_index([part, others[2 + i], others[i], others[4 + i]], axis),
                axis=("x", "y").index(axis),
            )
            for i, (part, axis) in enumerate(zip(parts, axes))
        ]
    parts = [part.reshape((-1,) + part.shape[2:]) for part in parts]
    return jnp.concatenate(parts, axis=1)


def slope(gradient, packed, width):
    unit = packed[:, :width].astype(jnp.float32)
    length = vector_of(packed[:, width:], 0)
    along = jnp.sum(unit * gradient, axis=1, keepdims=True)
    value = (gradient - unit * along) / length
    high = rounded(value)
    return high.astype(jnp.bfloat16), (value - high).astype(jnp.bfloat16)


def over_rows(features, slopes):
    return sum(
        lax.dot_general(
            features, part, (((0,), (0,)), ((), ())), preferred_element_type=jnp.float32
        )
        for part in slopes
    )


def per_device(image_x, text_x, image_gain, text_gain, image_w, text_w, sharpness, offset):
    scale, bias = sharpness[0], offset[0]
    towers = lax.axis_size("t")
    rows, width = image_x.shape[0], image_w.shape[1]
    image_values = image_x.astype(jnp.float32)
    text_values = text_x.astype(jnp.float32)
    moments = jnp.stack(
        [
            jnp.sum(image_values, axis=1),
            jnp.sum(image_values * image_values, axis=1),
            jnp.sum(text_values, axis=1),
            jnp.sum(text_values * text_values, axis=1),
        ]
    )
    moments, text_0, image_0 = tied(moments, text_x, image_x)
    moments_1 = swap(moments, "t")
    text_1, image_y = swap(text_0, "x", 1), swap(image_0, "y", 3)
    image_z = [swap(image_0, "z", k) for k in (1, 2, 3)]
    moments_1, text_1, image_y, image_z = tied(moments_1, text_1, image_y, image_z)
    moments = moments + moments_1
    image_scales = row_scales(moments[0], moments[1], image_x.shape[1] * towers)
    text_scales = row_scales(moments[2], moments[3], text_x.shape[1] * towers)
    image_part = jnp.dot(
        normed(image_x, *[v[:, None] for v in image_scales], image_gain),
        image_w,
        preferred_element_type=jnp.float32,
    )
    text_part = jnp.dot(
        normed(text_x, *[v[:, None] for v in text_scales], text_gain),
        text_w,
        preferred_element_type=jnp.float32,
    )
    text_2, image_z = jnp.concatenate([text_x, text_1], axis=0), jnp.concatenate(image_z, axis=0)
    image_far = swap(image_z, "y", 3)
    image_send, image_norm = unit_scaled(image_part)
    text_send, text_norm = unit_scaled(text_part)
    norms, image_send, text_send, text_3 = tied(
        jnp.stack([image_norm, text_norm]), image_send, text_send, swap(text_2, "x", 3)
    )
    image_other, text_other = swap(image_send, "t"), swap(text_send, "t")
    norms = swap(norms, "t")
    text_4 = jnp.concatenate([text_2, text_3], axis=0)
    text_8 = jnp.concatenate([text_4, swap(text_4, "y", 1)], axis=0)
    norms, text_other, image_other, text_8, image_far = tied(
        norms, text_other, image_other, text_8, image_far
    )
    image_pre = image_part + image_other.astype(jnp.float32) * norms[0][:, None]
    text_pre = text_part + text_other.astype(jnp.float32) * norms[1][:, None]
    text_rows, image_rows = gather_rows(
        packed_rows(text_pre, *text_scales), packed_rows(image_pre, *image_scales)
    )
    image_features = jnp.concatenate([image_x, image_z, image_y, image_far], axis=0)
    chips = text_8.reshape(2, 2, 2, 2, rows // 2, text_x.shape[1])
    text_features = both_cores(
        jnp.concatenate(
            [
                chips[:, :, :, 0].reshape(-1, text_x.shape[1]),
                chips[:, :, :, 1].transpose(1, 2, 0, 3, 4).reshape(-1, text_x.shape[1]),
            ],
            axis=0,
        )
    )
    image_normed_rows, text_normed_rows = (
        normed(features, vector_of(block, 1), vector_of(block, 2), gain)
        for features, block, gain in (
            (image_features, image_rows[:, width:], image_gain),
            (text_features, text_rows[:, width:], text_gain),
        )
    )

    image_units, text_units = image_rows[:, :width], text_rows[:, :width]
    products = lax.dot_general(
        image_units, text_units, (((1,), (1,)), ((), ())), preferred_element_type=jnp.float32
    )
    logits = scale * products + bias
    half = rows // 2
    row_ids = lax.broadcasted_iota(jnp.int32, products.shape, 0)
    column_ids = lax.broadcasted_iota(jnp.int32, products.shape, 1)
    same = ((column_ids == row_ids) & (row_ids < half)) | (
        (column_ids == row_ids + 7 * half) & (row_ids >= half) & (row_ids < rows)
    )
    labels = jnp.where(same, 1.0, -1.0).astype(jnp.float32)
    weights = (-labels * jax.nn.sigmoid(-labels * logits)).astype(jnp.bfloat16)
    image_grad = scale * jnp.dot(weights, text_units, preferred_element_type=jnp.float32)
    text_grad = scale * lax.dot_general(
        weights, image_units, (((0,), (0,)), ((), ())), preferred_element_type=jnp.float32
    )
    image_slope = slope(image_grad, image_rows, width)
    text_slope = slope(text_grad, text_rows, width)
    first = lax.axis_index("c") == 0

    def over_cores(term):
        lower, upper = jnp.split(term, 2, axis=0)
        return jnp.where(first, lower, upper) + swap(jnp.where(first, upper, lower), "c")

    image_kept = over_cores(over_rows(image_normed_rows, image_slope))
    text_kept = over_cores(over_rows(text_normed_rows, text_slope))
    plane = lax.axis_size("x") * lax.axis_size("y")
    image_deep, text_deep = image_w.shape[0] // 2, text_w.shape[0] // 2
    deep = image_deep + text_deep
    each = -(-deep // (plane * 16)) * 16
    kept = jnp.concatenate(
        [image_kept, text_kept, jnp.zeros((plane * each - deep, width), jnp.float32)], axis=0
    )
    blocks = kept.astype(jnp.bfloat16).reshape(plane, each, width)
    blocks = lax.all_to_all(blocks, ("x", "y"), 0, 0)
    block = rounded(jnp.sum(blocks.astype(jnp.float32), axis=0))
    others = tied(*[swap(block.astype(jnp.bfloat16), "z", k) for k in (2, 3, 1)])
    z2, z3, z1 = [other.astype(jnp.float32) for other in others]
    block = ((block + z1) + (z2 + z3)).astype(jnp.bfloat16)
    block = gather_xy(block).reshape(plane * each, width)
    other = swap(block, "c")
    lower, upper = jnp.where(first, block, other), jnp.where(first, other, block)
    return tuple(
        jnp.concatenate([lower[rows], upper[rows]], axis=0).astype(jnp.float32)
        for rows in (slice(0, image_deep), slice(image_deep, deep))
    )


def solution(mesh):
    grid = Mesh(mesh.devices.reshape(2, 4, 4, 4, 2), AXES)
    return jax.shard_map(
        per_device,
        mesh=grid,
        in_specs=(
            P(DP, "t"),
            P(DP, "t"),
            P("t"),
            P("t"),
            P("t", None),
            P("t", None),
            P(),
            P(),
        ),
        out_specs=(P("t", None), P("t", None)),
        check_vma=False,
    )
```

```python
import jax
import jax.numpy as jnp
from jax import lax
from jax.sharding import Mesh, PartitionSpec as P

AXES = ("t", "z", "x", "y", "c")
DP = ("z", "x", "y", "c")


def swap(x, axis, mask=1):
    return lax.ppermute(x, axis, [(i, i ^ mask) for i in range(lax.axis_size(axis))])


def row_scales(sums, squares, width):
    average = sums / width
    return average, lax.rsqrt(squares / width - average * average + 1e-06)


def normed(values, average, inverse, gain):
    values = values.astype(jnp.float32)
    return ((values - average) * inverse * gain[None, :]).astype(jnp.bfloat16)


def rounded(x):
    return lax.reduce_precision(x, 8, 7)


def columns_of(vectors, count=128):
    column = lax.broadcasted_iota(jnp.int32, (vectors[0].shape[0], count), 1)
    block = jnp.zeros(column.shape, jnp.float32)
    for i, rest in enumerate(vectors):
        for k in range(3):
            piece = rounded(rest)
            block = jnp.where(column == 3 * i + k, piece[:, None], block)
            rest = rest - piece
    return block.astype(jnp.bfloat16)


def vector_of(block, i):
    return jnp.sum(block[:, 3 * i : 3 * i + 3].astype(jnp.float32), axis=1, keepdims=True)


def float16_rows(*parts):
    column = lax.broadcasted_iota(jnp.int32, (parts[0].shape[0], 128), 1)
    exponents = jnp.zeros(column.shape, jnp.float32)
    scaled = []
    for i, part in enumerate(parts):
        square = jnp.mean(part * part, axis=1, keepdims=True)
        exponent = jnp.round(0.5 * jnp.log2(square + 1e-30))
        exponents = jnp.where(column == i, exponent, exponents)
        scaled.append(part * jnp.exp2(-exponent))
    return jnp.concatenate(scaled + [exponents], axis=1).astype(jnp.float16)


def from_float16(rows, width):
    exponents = rows[:, 2 * width :].astype(jnp.float32)
    return [
        rows[:, i * width : (i + 1) * width].astype(jnp.float32) * jnp.exp2(exponents[:, i : i + 1])
        for i in range(2)
    ]


def packed_rows(projected, average, inverse):
    length = jnp.sqrt(jnp.sum(projected * projected, axis=1, keepdims=True) + 1e-06)
    unit = (projected / length).astype(jnp.bfloat16)
    return jnp.concatenate([unit, columns_of([length[:, 0], average, inverse])], axis=1)


def tied(*arrays):
    return lax.optimization_barrier(arrays)


def gather_rows(text, image, text_2, image_4):
    low, high = jnp.split(text, 2, axis=0)
    image_z = [swap(image, "z", k) for k in (1, 2, 3)]
    low_1, high_1, near, text_2b = tied(
        swap(low, "x", 1), swap(high, "y", 1), image_z[0], swap(text_2, "x", 3)
    )
    text_4 = jnp.concatenate([text_2, text_2b], axis=0)
    image_y = [swap(image, "y", 3), swap(near, "y", 3)]
    low, high = jnp.concatenate([low, low_1], axis=0), jnp.concatenate([high, high_1], axis=0)
    low_1, high_1, text_4b, *image_z = tied(
        swap(low, "x", 3), swap(high, "x", 1), swap(text_4, "y", 1), *image_z[1:]
    )
    text_8 = jnp.concatenate([text_4, text_4b], axis=0)
    image_4b = swap(image_4, "y", 3)
    far = jnp.concatenate(image_z, axis=0)
    low, high = jnp.concatenate([low, low_1], axis=0), jnp.concatenate([high, high_1], axis=0)
    low_1, high_1, *image_y = tied(swap(low, "y", 1), swap(high, "x", 3), *image_y, swap(far, "y", 3))
    text = both_cores(jnp.concatenate([low, low_1, high, high_1], axis=0))
    image = jnp.concatenate([image, near, far] + image_y, axis=0)
    return text, image, text_8, jnp.concatenate([image_4, image_4b], axis=0)


def both_cores(x):
    return jnp.concatenate([x, swap(x, "c")], axis=0)


def by_index(parts, axis):
    index = lax.axis_index(axis)
    even, low = index % 2 == 0, index < 2
    pairs = [
        [jnp.where(even, a, b), jnp.where(even, b, a)] for a, b in (parts[:2], parts[2:])
    ]
    return [jnp.where(low, a, b) for a, b in zip(*pairs)] + [
        jnp.where(low, b, a) for a, b in zip(*pairs)
    ]


def gather_xy(block):
    parts = [part[None, None] for part in jnp.split(block, 2, axis=0)]
    for axes in (("x", "y"), ("y", "x")):
        others = tied(
            *[swap(part, axis, k) for k in (2, 1, 3) for part, axis in zip(parts, axes)]
        )
        parts = [
            jnp.concatenate(
                by_index([part, others[2 + i], others[i], others[4 + i]], axis),
                axis=("x", "y").index(axis),
            )
            for i, (part, axis) in enumerate(zip(parts, axes))
        ]
    parts = [part.reshape((-1,) + part.shape[2:]) for part in parts]
    return jnp.concatenate(parts, axis=1)


def slope(gradient, packed, width):
    unit = packed[:, :width].astype(jnp.float32)
    length = vector_of(packed[:, width:], 0)
    along = jnp.sum(unit * gradient, axis=1, keepdims=True)
    value = (gradient - unit * along) / length
    high = rounded(value)
    return high.astype(jnp.bfloat16), (value - high).astype(jnp.bfloat16)


def over_rows(features, slopes):
    return sum(
        lax.dot_general(
            features, part, (((0,), (0,)), ((), ())), preferred_element_type=jnp.float32
        )
        for part in slopes
    )


def per_device(image_x, text_x, image_gain, text_gain, image_w, text_w, sharpness, offset):
    scale, bias = sharpness[0], offset[0]
    towers = lax.axis_size("t")
    rows, width = image_x.shape[0], image_w.shape[1]
    image_values = image_x.astype(jnp.float32)
    text_values = text_x.astype(jnp.float32)
    moments = lax.psum(
        (
            jnp.sum(image_values, axis=1),
            jnp.sum(image_values * image_values, axis=1),
            jnp.sum(text_values, axis=1),
            jnp.sum(text_values * text_values, axis=1),
        ),
        "t",
    )
    image_scales = row_scales(moments[0], moments[1], image_x.shape[1] * towers)
    text_scales = row_scales(moments[2], moments[3], text_x.shape[1] * towers)
    image_part = jnp.dot(
        normed(image_x, *[v[:, None] for v in image_scales], image_gain),
        image_w,
        preferred_element_type=jnp.float32,
    )
    text_part = jnp.dot(
        normed(text_x, *[v[:, None] for v in text_scales], text_gain),
        text_w,
        preferred_element_type=jnp.float32,
    )
    send, text_0, image_0 = tied(float16_rows(image_part, text_part), text_x, image_x)
    other, text_1, *image_z = tied(
        swap(send, "t"), swap(text_0, "x", 1), *[swap(image_0, "z", k) for k in (1, 2, 3)]
    )
    image_other, text_other = from_float16(other, width)
    text_rows, image_rows, text_8, image_features = gather_rows(
        packed_rows(text_part + text_other, *text_scales),
        packed_rows(image_part + image_other, *image_scales),
        jnp.concatenate([text_x, text_1], axis=0),
        jnp.concatenate([image_x] + image_z, axis=0),
    )
    chips = text_8.reshape(2, 2, 2, 2, rows // 2, text_x.shape[1])
    text_features = both_cores(
        jnp.concatenate(
            [
                chips[:, :, :, 0].reshape(-1, text_x.shape[1]),
                chips[:, :, :, 1].transpose(1, 2, 0, 3, 4).reshape(-1, text_x.shape[1]),
            ],
            axis=0,
        )
    )
    image_normed_rows, text_normed_rows = (
        normed(features, vector_of(block, 1), vector_of(block, 2), gain)
        for features, block, gain in (
            (image_features, image_rows[:, width:], image_gain),
            (text_features, text_rows[:, width:], text_gain),
        )
    )

    image_units, text_units = image_rows[:, :width], text_rows[:, :width]
    products = lax.dot_general(
        image_units, text_units, (((1,), (1,)), ((), ())), preferred_element_type=jnp.float32
    )
    logits = scale * products + bias
    half = rows // 2
    row_ids = lax.broadcasted_iota(jnp.int32, products.shape, 0)
    column_ids = lax.broadcasted_iota(jnp.int32, products.shape, 1)
    same = ((column_ids == row_ids) & (row_ids < half)) | (
        (column_ids == row_ids + 7 * half) & (row_ids >= half) & (row_ids < rows)
    )
    labels = jnp.where(same, 1.0, -1.0).astype(jnp.float32)
    weights = (-labels * jax.nn.sigmoid(-labels * logits)).astype(jnp.bfloat16)
    image_grad = scale * jnp.dot(weights, text_units, preferred_element_type=jnp.float32)
    text_grad = scale * lax.dot_general(
        weights, image_units, (((0,), (0,)), ((), ())), preferred_element_type=jnp.float32
    )
    image_slope = slope(image_grad, image_rows, width)
    text_slope = slope(text_grad, text_rows, width)
    first = lax.axis_index("c") == 0

    def over_cores(term):
        lower, upper = jnp.split(term, 2, axis=0)
        return jnp.where(first, lower, upper) + swap(jnp.where(first, upper, lower), "c")

    image_kept = over_cores(over_rows(image_normed_rows, image_slope))
    text_kept = over_cores(over_rows(text_normed_rows, text_slope))
    plane = lax.axis_size("x") * lax.axis_size("y")
    image_deep, text_deep = image_w.shape[0] // 2, text_w.shape[0] // 2
    deep = image_deep + text_deep
    each = -(-deep // (plane * 16)) * 16
    kept = jnp.concatenate(
        [image_kept, text_kept, jnp.zeros((plane * each - deep, width), jnp.float32)], axis=0
    )
    blocks = kept.astype(jnp.bfloat16).reshape(plane, each, width)
    blocks = lax.all_to_all(blocks, ("x", "y"), 0, 0)
    block = rounded(jnp.sum(blocks.astype(jnp.float32), axis=0))
    others = tied(*[swap(block.astype(jnp.bfloat16), "z", k) for k in (2, 3, 1)])
    z2, z3, z1 = [other.astype(jnp.float32) for other in others]
    block = ((block + z1) + (z2 + z3)).astype(jnp.bfloat16)
    block = gather_xy(block).reshape(plane * each, width)
    other = swap(block, "c")
    lower, upper = jnp.where(first, block, other), jnp.where(first, other, block)
    return tuple(
        jnp.concatenate([lower[rows], upper[rows]], axis=0).astype(jnp.float32)
        for rows in (slice(0, image_deep), slice(image_deep, deep))
    )


def solution(mesh):
    grid = Mesh(mesh.devices.reshape(2, 4, 4, 4, 2), AXES)
    return jax.shard_map(
        per_device,
        mesh=grid,
        in_specs=(
            P(DP, "t"),
            P(DP, "t"),
            P("t"),
            P("t"),
            P("t", None),
            P("t", None),
            P(),
            P(),
        ),
        out_specs=(P("t", None), P("t", None)),
        check_vma=False,
    )
```

```python
import jax
import jax.numpy as jnp
from jax import lax
from jax.sharding import Mesh, PartitionSpec as P

AXES = ("t", "z", "x", "y", "c")
DP = ("z", "x", "y", "c")


def swap(x, axis, mask=1):
    return lax.ppermute(x, axis, [(i, i ^ mask) for i in range(lax.axis_size(axis))])


def row_scales(sums, squares, width):
    average = sums / width
    return average, lax.rsqrt(squares / width - average * average + 1e-06)


def normed(values, average, inverse, gain):
    values = values.astype(jnp.float32)
    return ((values - average) * inverse * gain[None, :]).astype(jnp.bfloat16)


def rounded(x):
    return lax.reduce_precision(x, 8, 7)


def columns_of(vectors, count=128):
    column = lax.broadcasted_iota(jnp.int32, (vectors[0].shape[0], count), 1)
    block = jnp.zeros(column.shape, jnp.float32)
    for i, rest in enumerate(vectors):
        for k in range(3):
            piece = rounded(rest)
            block = jnp.where(column == 3 * i + k, piece[:, None], block)
            rest = rest - piece
    return block.astype(jnp.bfloat16)


def vector_of(block, i):
    return jnp.sum(block[:, 3 * i : 3 * i + 3].astype(jnp.float32), axis=1, keepdims=True)


def float16_rows(*parts):
    column = lax.broadcasted_iota(jnp.int32, (parts[0].shape[0], 128), 1)
    exponents = jnp.zeros(column.shape, jnp.float32)
    scaled = []
    for i, part in enumerate(parts):
        square = jnp.mean(part * part, axis=1, keepdims=True)
        exponent = jnp.round(0.5 * jnp.log2(square + 1e-30))
        exponents = jnp.where(column == i, exponent, exponents)
        scaled.append(part * jnp.exp2(-exponent))
    return jnp.concatenate(scaled + [exponents], axis=1).astype(jnp.float16)


def from_float16(rows, width):
    exponents = rows[:, 2 * width :].astype(jnp.float32)
    return [
        rows[:, i * width : (i + 1) * width].astype(jnp.float32) * jnp.exp2(exponents[:, i : i + 1])
        for i in range(2)
    ]


def packed_rows(projected, average, inverse):
    length = jnp.sqrt(jnp.sum(projected * projected, axis=1, keepdims=True) + 1e-06)
    unit = (projected / length).astype(jnp.bfloat16)
    return jnp.concatenate([unit, columns_of([length[:, 0], average, inverse])], axis=1)


def tied(*arrays):
    return lax.optimization_barrier(arrays)


def gather_rows(text, image, text_2):
    low, high = jnp.split(text, 2, axis=0)
    image_z = [swap(image, "z", k) for k in (1, 2, 3)]
    low_1, high_1, near, text_2b = tied(
        swap(low, "x", 1), swap(high, "y", 1), image_z[0], swap(text_2, "x", 3)
    )
    text_4 = jnp.concatenate([text_2, text_2b], axis=0)
    image_y = [swap(image, "y", 3), swap(near, "y", 3)]
    low, high = jnp.concatenate([low, low_1], axis=0), jnp.concatenate([high, high_1], axis=0)
    low_1, high_1, text_4b, *image_z = tied(
        swap(low, "x", 3), swap(high, "x", 1), swap(text_4, "y", 1), *image_z[1:]
    )
    text_8 = jnp.concatenate([text_4, text_4b], axis=0)
    far = jnp.concatenate(image_z, axis=0)
    low, high = jnp.concatenate([low, low_1], axis=0), jnp.concatenate([high, high_1], axis=0)
    low_1, high_1, *image_y = tied(swap(low, "y", 1), swap(high, "x", 3), *image_y, swap(far, "y", 3))
    text = both_cores(jnp.concatenate([low, low_1, high, high_1], axis=0))
    image = jnp.concatenate([image, near, far] + image_y, axis=0)
    return text, image, text_8


def both_cores(x):
    return jnp.concatenate([x, swap(x, "c")], axis=0)


def by_index(parts, axis):
    index = lax.axis_index(axis)
    even, low = index % 2 == 0, index < 2
    pairs = [
        [jnp.where(even, a, b), jnp.where(even, b, a)] for a, b in (parts[:2], parts[2:])
    ]
    return [jnp.where(low, a, b) for a, b in zip(*pairs)] + [
        jnp.where(low, b, a) for a, b in zip(*pairs)
    ]


def gather_xy(block):
    parts = [part[None, None] for part in jnp.split(block, 2, axis=0)]
    for axes in (("x", "y"), ("y", "x")):
        others = tied(
            *[swap(part, axis, k) for k in (2, 1, 3) for part, axis in zip(parts, axes)]
        )
        parts = [
            jnp.concatenate(
                by_index([part, others[2 + i], others[i], others[4 + i]], axis),
                axis=("x", "y").index(axis),
            )
            for i, (part, axis) in enumerate(zip(parts, axes))
        ]
    parts = [part.reshape((-1,) + part.shape[2:]) for part in parts]
    return jnp.concatenate(parts, axis=1)


def slope(gradient, packed, width):
    unit = packed[:, :width].astype(jnp.float32)
    length = vector_of(packed[:, width:], 0)
    along = jnp.sum(unit * gradient, axis=1, keepdims=True)
    value = (gradient - unit * along) / length
    high = rounded(value)
    return high.astype(jnp.bfloat16), (value - high).astype(jnp.bfloat16)


def over_rows(features, slopes):
    return sum(
        lax.dot_general(
            features, part, (((0,), (0,)), ((), ())), preferred_element_type=jnp.float32
        )
        for part in slopes
    )


def per_device(image_x, text_x, image_gain, text_gain, image_w, text_w, sharpness, offset):
    scale, bias = sharpness[0], offset[0]
    towers = lax.axis_size("t")
    rows, width = image_x.shape[0], image_w.shape[1]
    image_values = image_x.astype(jnp.float32)
    text_values = text_x.astype(jnp.float32)
    moments = lax.psum(
        (
            jnp.sum(image_values, axis=1),
            jnp.sum(image_values * image_values, axis=1),
            jnp.sum(text_values, axis=1),
            jnp.sum(text_values * text_values, axis=1),
        ),
        "t",
    )
    moments, *image_z = tied(moments, *[swap(image_x, "z", k) for k in (1, 2, 3)])
    image_4 = jnp.concatenate([image_x] + image_z, axis=0)
    image_scales = row_scales(moments[0], moments[1], image_x.shape[1] * towers)
    text_scales = row_scales(moments[2], moments[3], text_x.shape[1] * towers)
    image_part = jnp.dot(
        normed(image_x, *[v[:, None] for v in image_scales], image_gain),
        image_w,
        preferred_element_type=jnp.float32,
    )
    text_part = jnp.dot(
        normed(text_x, *[v[:, None] for v in text_scales], text_gain),
        text_w,
        preferred_element_type=jnp.float32,
    )
    send, text_0, image_4 = tied(float16_rows(image_part, text_part), text_x, image_4)
    other, text_1, image_4b = tied(
        swap(send, "t"), swap(text_0, "x", 1), swap(image_4, "y", 3)
    )
    image_other, text_other = from_float16(other, width)
    text_rows, image_rows, text_8 = gather_rows(
        packed_rows(text_part + text_other, *text_scales),
        packed_rows(image_part + image_other, *image_scales),
        jnp.concatenate([text_x, text_1], axis=0),
    )
    image_features = jnp.concatenate([image_4, image_4b], axis=0)
    chips = text_8.reshape(2, 2, 2, 2, rows // 2, text_x.shape[1])
    text_features = both_cores(
        jnp.concatenate(
            [
                chips[:, :, :, 0].reshape(-1, text_x.shape[1]),
                chips[:, :, :, 1].transpose(1, 2, 0, 3, 4).reshape(-1, text_x.shape[1]),
            ],
            axis=0,
        )
    )
    image_normed_rows, text_normed_rows = (
        normed(features, vector_of(block, 1), vector_of(block, 2), gain)
        for features, block, gain in (
            (image_features, image_rows[:, width:], image_gain),
            (text_features, text_rows[:, width:], text_gain),
        )
    )

    image_units, text_units = image_rows[:, :width], text_rows[:, :width]
    products = lax.dot_general(
        image_units, text_units, (((1,), (1,)), ((), ())), preferred_element_type=jnp.float32
    )
    logits = scale * products + bias
    half = rows // 2
    row_ids = lax.broadcasted_iota(jnp.int32, products.shape, 0)
    column_ids = lax.broadcasted_iota(jnp.int32, products.shape, 1)
    same = ((column_ids == row_ids) & (row_ids < half)) | (
        (column_ids == row_ids + 7 * half) & (row_ids >= half) & (row_ids < rows)
    )
    labels = jnp.where(same, 1.0, -1.0).astype(jnp.float32)
    weights = (-labels * jax.nn.sigmoid(-labels * logits)).astype(jnp.bfloat16)
    image_grad = scale * jnp.dot(weights, text_units, preferred_element_type=jnp.float32)
    text_grad = scale * lax.dot_general(
        weights, image_units, (((0,), (0,)), ((), ())), preferred_element_type=jnp.float32
    )
    image_slope = slope(image_grad, image_rows, width)
    text_slope = slope(text_grad, text_rows, width)
    first = lax.axis_index("c") == 0

    def over_cores(term):
        lower, upper = jnp.split(term, 2, axis=0)
        return jnp.where(first, lower, upper) + swap(jnp.where(first, upper, lower), "c")

    image_kept = over_cores(over_rows(image_normed_rows, image_slope))
    text_kept = over_cores(over_rows(text_normed_rows, text_slope))
    plane = lax.axis_size("x") * lax.axis_size("y")
    image_deep, text_deep = image_w.shape[0] // 2, text_w.shape[0] // 2
    deep = image_deep + text_deep
    each = -(-deep // (plane * 16)) * 16
    kept = jnp.concatenate(
        [image_kept, text_kept, jnp.zeros((plane * each - deep, width), jnp.float32)], axis=0
    )
    blocks = kept.astype(jnp.bfloat16).reshape(plane, each, width)
    blocks = lax.all_to_all(blocks, ("x", "y"), 0, 0)
    block = rounded(jnp.sum(blocks.astype(jnp.float32), axis=0))
    others = tied(*[swap(block.astype(jnp.bfloat16), "z", k) for k in (2, 3, 1)])
    z2, z3, z1 = [other.astype(jnp.float32) for other in others]
    block = ((block + z1) + (z2 + z3)).astype(jnp.bfloat16)
    block = gather_xy(block).reshape(plane * each, width)
    other = swap(block, "c")
    lower, upper = jnp.where(first, block, other), jnp.where(first, other, block)
    return tuple(
        jnp.concatenate([lower[rows], upper[rows]], axis=0).astype(jnp.float32)
        for rows in (slice(0, image_deep), slice(image_deep, deep))
    )


def solution(mesh):
    grid = Mesh(mesh.devices.reshape(2, 4, 4, 4, 2), AXES)
    return jax.shard_map(
        per_device,
        mesh=grid,
        in_specs=(
            P(DP, "t"),
            P(DP, "t"),
            P("t"),
            P("t"),
            P("t", None),
            P("t", None),
            P(),
            P(),
        ),
        out_specs=(P("t", None), P("t", None)),
        check_vma=False,
    )
```

```python
import jax
import jax.numpy as jnp
from jax import lax
from jax.sharding import Mesh, PartitionSpec as P

AXES = ("t", "z", "x", "y", "c")
DP = ("z", "x", "y", "c")


def swap(x, axis, mask=1):
    return lax.ppermute(x, axis, [(i, i ^ mask) for i in range(lax.axis_size(axis))])


def row_scales(sums, squares, width):
    average = sums / width
    return average, lax.rsqrt(squares / width - average * average + 1e-06)


def normed(values, average, inverse, gain):
    values = values.astype(jnp.float32)
    return ((values - average) * inverse * gain[None, :]).astype(jnp.bfloat16)


def rounded(x):
    return lax.reduce_precision(x, 8, 7)


def columns_of(vectors, count=128):
    column = lax.broadcasted_iota(jnp.int32, (vectors[0].shape[0], count), 1)
    block = jnp.zeros(column.shape, jnp.float32)
    for i, rest in enumerate(vectors):
        for k in range(3):
            piece = rounded(rest)
            block = jnp.where(column == 3 * i + k, piece[:, None], block)
            rest = rest - piece
    return block.astype(jnp.bfloat16)


def vector_of(block, i):
    return jnp.sum(block[:, 3 * i : 3 * i + 3].astype(jnp.float32), axis=1, keepdims=True)


def float16_rows(*parts):
    column = lax.broadcasted_iota(jnp.int32, (parts[0].shape[0], 128), 1)
    exponents = jnp.zeros(column.shape, jnp.float32)
    scaled = []
    for i, part in enumerate(parts):
        square = jnp.mean(part * part, axis=1, keepdims=True)
        exponent = jnp.round(0.5 * jnp.log2(square + 1e-30))
        exponents = jnp.where(column == i, exponent, exponents)
        scaled.append(part * jnp.exp2(-exponent))
    return jnp.concatenate(scaled + [exponents], axis=1).astype(jnp.float16)


def from_float16(rows, width):
    exponents = rows[:, 2 * width :].astype(jnp.float32)
    return [
        rows[:, i * width : (i + 1) * width].astype(jnp.float32) * jnp.exp2(exponents[:, i : i + 1])
        for i in range(2)
    ]


def packed_rows(projected, average, inverse):
    length = jnp.sqrt(jnp.sum(projected * projected, axis=1, keepdims=True) + 1e-06)
    unit = (projected / length).astype(jnp.bfloat16)
    return jnp.concatenate([unit, columns_of([length[:, 0], average, inverse])], axis=1)


def tied(*arrays):
    return lax.optimization_barrier(arrays)


def gather_rows(text, image, text_2):
    low, high = jnp.split(text, 2, axis=0)
    image_z = [swap(image, "z", k) for k in (1, 2, 3)]
    low_1, high_1, near, text_2b = tied(
        swap(low, "x", 1), swap(high, "y", 1), image_z[0], swap(text_2, "x", 3)
    )
    text_4 = jnp.concatenate([text_2, text_2b], axis=0)
    image = jnp.concatenate([image, near], axis=0)
    image_y = swap(image, "y", 3)
    low, high = jnp.concatenate([low, low_1], axis=0), jnp.concatenate([high, high_1], axis=0)
    low_1, high_1, text_4b, *image_z = tied(
        swap(low, "x", 3), swap(high, "x", 1), swap(text_4, "y", 1), *image_z[1:]
    )
    text_8 = jnp.concatenate([text_4, text_4b], axis=0)
    far = jnp.concatenate(image_z, axis=0)
    low, high = jnp.concatenate([low, low_1], axis=0), jnp.concatenate([high, high_1], axis=0)
    first = jnp.concatenate([low, high], axis=0)
    first_c, low, high, image_y, far_y, text_8 = tied(
        swap(first, "c"), swap(low, "y", 1), swap(high, "x", 3), image_y, swap(far, "y", 3), text_8
    )
    second = jnp.concatenate([low, high], axis=0)
    text = jnp.concatenate([first, second, first_c, swap(second, "c")], axis=0)
    image = jnp.concatenate([image, far, image_y, far_y], axis=0)
    return text, image, text_8


def both_cores(x):
    return jnp.concatenate([x, swap(x, "c")], axis=0)


def by_index(parts, axis):
    index = lax.axis_index(axis)
    even, low = index % 2 == 0, index < 2
    pairs = [
        [jnp.where(even, a, b), jnp.where(even, b, a)] for a, b in (parts[:2], parts[2:])
    ]
    return [jnp.where(low, a, b) for a, b in zip(*pairs)] + [
        jnp.where(low, b, a) for a, b in zip(*pairs)
    ]


def gather_xy(block):
    parts = [part[None, None] for part in jnp.split(block, 2, axis=0)]
    for axes in (("x", "y"), ("y", "x")):
        others = tied(
            *[swap(part, axis, k) for k in (2, 1, 3) for part, axis in zip(parts, axes)]
        )
        parts = [
            jnp.concatenate(
                by_index([part, others[2 + i], others[i], others[4 + i]], axis),
                axis=("x", "y").index(axis),
            )
            for i, (part, axis) in enumerate(zip(parts, axes))
        ]
    parts = [part.reshape((-1,) + part.shape[2:]) for part in parts]
    return jnp.concatenate(parts, axis=1)


def slope(gradient, packed, width):
    unit = packed[:, :width].astype(jnp.float32)
    length = vector_of(packed[:, width:], 0)
    along = jnp.sum(unit * gradient, axis=1, keepdims=True)
    value = (gradient - unit * along) / length
    high = rounded(value)
    return high.astype(jnp.bfloat16), (value - high).astype(jnp.bfloat16)


def over_rows(features, slopes):
    return sum(
        lax.dot_general(
            features, part, (((0,), (0,)), ((), ())), preferred_element_type=jnp.float32
        )
        for part in slopes
    )


def per_device(image_x, text_x, image_gain, text_gain, image_w, text_w, sharpness, offset):
    scale, bias = sharpness[0], offset[0]
    towers = lax.axis_size("t")
    rows, width = image_x.shape[0], image_w.shape[1]
    image_values = image_x.astype(jnp.float32)
    text_values = text_x.astype(jnp.float32)
    moments = lax.psum(
        (
            jnp.sum(image_values, axis=1),
            jnp.sum(image_values * image_values, axis=1),
            jnp.sum(text_values, axis=1),
            jnp.sum(text_values * text_values, axis=1),
        ),
        "t",
    )
    moments, *image_z = tied(moments, *[swap(image_x, "z", k) for k in (1, 2, 3)])
    image_4 = jnp.concatenate([image_x] + image_z, axis=0)
    image_scales = row_scales(moments[0], moments[1], image_x.shape[1] * towers)
    text_scales = row_scales(moments[2], moments[3], text_x.shape[1] * towers)
    image_part = jnp.dot(
        normed(image_x, *[v[:, None] for v in image_scales], image_gain),
        image_w,
        preferred_element_type=jnp.float32,
    )
    text_part = jnp.dot(
        normed(text_x, *[v[:, None] for v in text_scales], text_gain),
        text_w,
        preferred_element_type=jnp.float32,
    )
    send, text_0, image_4 = tied(float16_rows(image_part, text_part), text_x, image_4)
    other, text_1, image_4b = tied(
        swap(send, "t"), swap(text_0, "x", 1), swap(image_4, "y", 3)
    )
    image_other, text_other = from_float16(other, width)
    text_rows, image_rows, text_8 = gather_rows(
        packed_rows(text_part + text_other, *text_scales),
        packed_rows(image_part + image_other, *image_scales),
        jnp.concatenate([text_x, text_1], axis=0),
    )
    image_features = jnp.concatenate([image_4, image_4b], axis=0)
    chips = text_8.reshape(2, 2, 2, 2, rows // 2, text_x.shape[1])
    quarters = []
    for k in range(2):
        quarters += [chips[k, :, :, 0], chips[:, k, :, 1].swapaxes(0, 1)]
    text_features = both_cores(
        jnp.concatenate([part.reshape(-1, text_x.shape[1]) for part in quarters], axis=0)
    )
    image_normed_rows, text_normed_rows = (
        normed(features, vector_of(block, 1), vector_of(block, 2), gain)
        for features, block, gain in (
            (image_features, image_rows[:, width:], image_gain),
            (text_features, text_rows[:, width:], text_gain),
        )
    )

    image_units, text_units = image_rows[:, :width], text_rows[:, :width]
    products = lax.dot_general(
        image_units, text_units, (((1,), (1,)), ((), ())), preferred_element_type=jnp.float32
    )
    logits = scale * products + bias
    half = rows // 2
    row_ids = lax.broadcasted_iota(jnp.int32, products.shape, 0)
    column_ids = lax.broadcasted_iota(jnp.int32, products.shape, 1)
    same = ((column_ids == row_ids) & (row_ids < half)) | (
        (column_ids == row_ids + 3 * half) & (row_ids >= half) & (row_ids < rows)
    )
    labels = jnp.where(same, 1.0, -1.0).astype(jnp.float32)
    weights = (-labels * jax.nn.sigmoid(-labels * logits)).astype(jnp.bfloat16)
    image_grad = scale * jnp.dot(weights, text_units, preferred_element_type=jnp.float32)
    text_grad = scale * lax.dot_general(
        weights, image_units, (((0,), (0,)), ((), ())), preferred_element_type=jnp.float32
    )
    image_slope = slope(image_grad, image_rows, width)
    text_slope = slope(text_grad, text_rows, width)
    first = lax.axis_index("c") == 0

    def over_cores(term):
        lower, upper = jnp.split(term, 2, axis=0)
        return jnp.where(first, lower, upper) + swap(jnp.where(first, upper, lower), "c")

    image_kept = over_cores(over_rows(image_normed_rows, image_slope))
    text_kept = over_cores(over_rows(text_normed_rows, text_slope))
    plane = lax.axis_size("x") * lax.axis_size("y")
    image_deep, text_deep = image_w.shape[0] // 2, text_w.shape[0] // 2
    deep = image_deep + text_deep
    each = -(-deep // (plane * 16)) * 16
    kept = jnp.concatenate(
        [image_kept, text_kept, jnp.zeros((plane * each - deep, width), jnp.float32)], axis=0
    )
    blocks = kept.astype(jnp.bfloat16).reshape(plane, each, width)
    blocks = lax.all_to_all(blocks, ("x", "y"), 0, 0)
    block = rounded(jnp.sum(blocks.astype(jnp.float32), axis=0))
    others = tied(*[swap(block.astype(jnp.bfloat16), "z", k) for k in (2, 3, 1)])
    z2, z3, z1 = [other.astype(jnp.float32) for other in others]
    block = ((block + z1) + (z2 + z3)).astype(jnp.bfloat16)
    block = gather_xy(block).reshape(plane * each, width)
    other = swap(block, "c")
    lower, upper = jnp.where(first, block, other), jnp.where(first, other, block)
    return tuple(
        jnp.concatenate([lower[rows], upper[rows]], axis=0).astype(jnp.float32)
        for rows in (slice(0, image_deep), slice(image_deep, deep))
    )


def solution(mesh):
    grid = Mesh(mesh.devices.reshape(2, 4, 4, 4, 2), AXES)
    return jax.shard_map(
        per_device,
        mesh=grid,
        in_specs=(
            P(DP, "t"),
            P(DP, "t"),
            P("t"),
            P("t"),
            P("t", None),
            P("t", None),
            P(),
            P(),
        ),
        out_specs=(P("t", None), P("t", None)),
        check_vma=False,
    )
```

```python
import jax
import jax.numpy as jnp
from jax import lax
from jax.sharding import Mesh, PartitionSpec as P

AXES = ("t", "z", "x", "y", "c")
DP = ("z", "x", "y", "c")


def swap(x, axis, mask=1):
    return lax.ppermute(x, axis, [(i, i ^ mask) for i in range(lax.axis_size(axis))])


def row_scales(sums, squares, width):
    average = sums / width
    return average, lax.rsqrt(squares / width - average * average + 1e-06)


def normed(values, average, inverse, gain):
    values = values.astype(jnp.float32)
    return ((values - average) * inverse * gain[None, :]).astype(jnp.bfloat16)


def rounded(x):
    return lax.reduce_precision(x, 8, 7)


def columns_of(vectors, count=128):
    column = lax.broadcasted_iota(jnp.int32, (vectors[0].shape[0], count), 1)
    block = jnp.zeros(column.shape, jnp.float32)
    for i, rest in enumerate(vectors):
        for k in range(3):
            piece = rounded(rest)
            block = jnp.where(column == 3 * i + k, piece[:, None], block)
            rest = rest - piece
    return block.astype(jnp.bfloat16)


def vector_of(block, i):
    return jnp.sum(block[:, 3 * i : 3 * i + 3].astype(jnp.float32), axis=1, keepdims=True)


def float16_rows(*parts):
    column = lax.broadcasted_iota(jnp.int32, (parts[0].shape[0], 128), 1)
    exponents = jnp.zeros(column.shape, jnp.float32)
    scaled = []
    for i, part in enumerate(parts):
        square = jnp.mean(part * part, axis=1, keepdims=True)
        exponent = jnp.round(0.5 * jnp.log2(square + 1e-30))
        exponents = jnp.where(column == i, exponent, exponents)
        scaled.append(part * jnp.exp2(-exponent))
    return jnp.concatenate(scaled + [exponents], axis=1).astype(jnp.float16)


def from_float16(rows, width):
    exponents = rows[:, 2 * width :].astype(jnp.float32)
    return [
        rows[:, i * width : (i + 1) * width].astype(jnp.float32) * jnp.exp2(exponents[:, i : i + 1])
        for i in range(2)
    ]


def packed_rows(projected, average, inverse):
    length = jnp.sqrt(jnp.sum(projected * projected, axis=1, keepdims=True) + 1e-06)
    unit = (projected / length).astype(jnp.bfloat16)
    return jnp.concatenate([unit, columns_of([length[:, 0], average, inverse])], axis=1)


def tied(*arrays):
    return lax.optimization_barrier(arrays)


def gather_rows(text, image, text_2, image_4):
    low, high = jnp.split(text, 2, axis=0)
    image_z = [swap(image, "z", k) for k in (1, 2, 3)]
    low_1, high_1, near, text_2b, own_y = tied(
        swap(low, "x", 1),
        swap(high, "y", 1),
        image_z[0],
        swap(text_2, "x", 3),
        swap(image, "y", 3),
    )
    text_4 = jnp.concatenate([text_2, text_2b], axis=0)
    low, high = jnp.concatenate([low, low_1], axis=0), jnp.concatenate([high, high_1], axis=0)
    low_1, high_1, text_4b, near_y, *image_z = tied(
        swap(low, "x", 3),
        swap(high, "x", 1),
        swap(text_4, "y", 1),
        swap(near, "y", 3),
        *image_z[1:],
    )
    text_8 = jnp.concatenate([text_4, text_4b], axis=0)
    far = jnp.concatenate(image_z, axis=0)
    low, high = jnp.concatenate([low, low_1], axis=0), jnp.concatenate([high, high_1], axis=0)
    first = jnp.concatenate([low, high], axis=0)
    first_c, low, high, text_8, image_4, far_y = tied(
        swap(first, "c"),
        swap(low, "y", 1),
        swap(high, "x", 3),
        text_8,
        image_4,
        swap(far, "y", 3),
    )
    second = jnp.concatenate([low, high], axis=0)
    text = jnp.concatenate([first, second, first_c, swap(second, "c")], axis=0)
    image = jnp.concatenate([image, near, far, own_y, near_y, far_y], axis=0)
    return text, image, text_8, jnp.concatenate([image_4, swap(image_4, "y", 3)], axis=0)


def both_cores(x):
    return jnp.concatenate([x, swap(x, "c")], axis=0)


def by_index(parts, axis):
    index = lax.axis_index(axis)
    even, low = index % 2 == 0, index < 2
    pairs = [
        [jnp.where(even, a, b), jnp.where(even, b, a)] for a, b in (parts[:2], parts[2:])
    ]
    return [jnp.where(low, a, b) for a, b in zip(*pairs)] + [
        jnp.where(low, b, a) for a, b in zip(*pairs)
    ]


def gather_xy(block):
    parts = [part[None, None] for part in jnp.split(block, 2, axis=0)]
    for axes in (("x", "y"), ("y", "x")):
        others = tied(
            *[swap(part, axis, k) for k in (2, 1, 3) for part, axis in zip(parts, axes)]
        )
        parts = [
            jnp.concatenate(
                by_index([part, others[2 + i], others[i], others[4 + i]], axis),
                axis=("x", "y").index(axis),
            )
            for i, (part, axis) in enumerate(zip(parts, axes))
        ]
    parts = [part.reshape((-1,) + part.shape[2:]) for part in parts]
    return jnp.concatenate(parts, axis=1)


def slope(gradient, packed, width):
    unit = packed[:, :width].astype(jnp.float32)
    length = vector_of(packed[:, width:], 0)
    along = jnp.sum(unit * gradient, axis=1, keepdims=True)
    value = (gradient - unit * along) / length
    high = rounded(value)
    return high.astype(jnp.bfloat16), (value - high).astype(jnp.bfloat16)


def over_rows(features, slopes):
    return sum(
        lax.dot_general(
            features, part, (((0,), (0,)), ((), ())), preferred_element_type=jnp.float32
        )
        for part in slopes
    )


def per_device(image_x, text_x, image_gain, text_gain, image_w, text_w, sharpness, offset):
    scale, bias = sharpness[0], offset[0]
    towers = lax.axis_size("t")
    rows, width = image_x.shape[0], image_w.shape[1]
    image_values = image_x.astype(jnp.float32)
    text_values = text_x.astype(jnp.float32)
    moments = lax.psum(
        (
            jnp.sum(image_values, axis=1),
            jnp.sum(image_values * image_values, axis=1),
            jnp.sum(text_values, axis=1),
            jnp.sum(text_values * text_values, axis=1),
        ),
        "t",
    )
    moments, *image_z = tied(moments, *[swap(image_x, "z", k) for k in (1, 2, 3)])
    image_4 = jnp.concatenate([image_x] + image_z, axis=0)
    image_scales = row_scales(moments[0], moments[1], image_x.shape[1] * towers)
    text_scales = row_scales(moments[2], moments[3], text_x.shape[1] * towers)
    image_part = jnp.dot(
        normed(image_x, *[v[:, None] for v in image_scales], image_gain),
        image_w,
        preferred_element_type=jnp.float32,
    )
    text_part = jnp.dot(
        normed(text_x, *[v[:, None] for v in text_scales], text_gain),
        text_w,
        preferred_element_type=jnp.float32,
    )
    send, text_0 = tied(float16_rows(image_part, text_part), text_x)
    other, text_1 = tied(swap(send, "t"), swap(text_0, "x", 1))
    image_other, text_other = from_float16(other, width)
    text_rows, image_rows, text_8, image_features = gather_rows(
        packed_rows(text_part + text_other, *text_scales),
        packed_rows(image_part + image_other, *image_scales),
        jnp.concatenate([text_x, text_1], axis=0),
        image_4,
    )
    chips = text_8.reshape(2, 2, 2, 2, rows // 2, text_x.shape[1])
    quarters = []
    for k in range(2):
        quarters += [chips[k, :, :, 0], chips[:, k, :, 1].swapaxes(0, 1)]
    text_features = both_cores(
        jnp.concatenate([part.reshape(-1, text_x.shape[1]) for part in quarters], axis=0)
    )
    image_normed_rows, text_normed_rows = (
        normed(features, vector_of(block, 1), vector_of(block, 2), gain)
        for features, block, gain in (
            (image_features, image_rows[:, width:], image_gain),
            (text_features, text_rows[:, width:], text_gain),
        )
    )

    image_units, text_units = image_rows[:, :width], text_rows[:, :width]
    products = lax.dot_general(
        image_units, text_units, (((1,), (1,)), ((), ())), preferred_element_type=jnp.float32
    )
    logits = scale * products + bias
    half = rows // 2
    row_ids = lax.broadcasted_iota(jnp.int32, products.shape, 0)
    column_ids = lax.broadcasted_iota(jnp.int32, products.shape, 1)
    same = ((column_ids == row_ids) & (row_ids < half)) | (
        (column_ids == row_ids + 3 * half) & (row_ids >= half) & (row_ids < rows)
    )
    labels = jnp.where(same, 1.0, -1.0).astype(jnp.float32)
    weights = (-labels * jax.nn.sigmoid(-labels * logits)).astype(jnp.bfloat16)
    image_grad = scale * jnp.dot(weights, text_units, preferred_element_type=jnp.float32)
    text_grad = scale * lax.dot_general(
        weights, image_units, (((0,), (0,)), ((), ())), preferred_element_type=jnp.float32
    )
    image_slope = slope(image_grad, image_rows, width)
    text_slope = slope(text_grad, text_rows, width)
    first = lax.axis_index("c") == 0

    def over_cores(term):
        lower, upper = jnp.split(term, 2, axis=0)
        return jnp.where(first, lower, upper) + swap(jnp.where(first, upper, lower), "c")

    image_kept = over_cores(over_rows(image_normed_rows, image_slope))
    text_kept = over_cores(over_rows(text_normed_rows, text_slope))
    plane = lax.axis_size("x") * lax.axis_size("y")
    image_deep, text_deep = image_w.shape[0] // 2, text_w.shape[0] // 2
    deep = image_deep + text_deep
    each = -(-deep // (plane * 16)) * 16
    kept = jnp.concatenate(
        [image_kept, text_kept, jnp.zeros((plane * each - deep, width), jnp.float32)], axis=0
    )
    blocks = kept.astype(jnp.bfloat16).reshape(plane, each, width)
    blocks = lax.all_to_all(blocks, ("x", "y"), 0, 0)
    block = rounded(jnp.sum(blocks.astype(jnp.float32), axis=0))
    others = tied(*[swap(block.astype(jnp.bfloat16), "z", k) for k in (2, 3, 1)])
    z2, z3, z1 = [other.astype(jnp.float32) for other in others]
    block = ((block + z1) + (z2 + z3)).astype(jnp.bfloat16)
    block = gather_xy(block).reshape(plane * each, width)
    other = swap(block, "c")
    lower, upper = jnp.where(first, block, other), jnp.where(first, other, block)
    return tuple(
        jnp.concatenate([lower[rows], upper[rows]], axis=0).astype(jnp.float32)
        for rows in (slice(0, image_deep), slice(image_deep, deep))
    )


def solution(mesh):
    grid = Mesh(mesh.devices.reshape(2, 4, 4, 4, 2), AXES)
    return jax.shard_map(
        per_device,
        mesh=grid,
        in_specs=(
            P(DP, "t"),
            P(DP, "t"),
            P("t"),
            P("t"),
            P("t", None),
            P("t", None),
            P(),
            P(),
        ),
        out_specs=(P("t", None), P("t", None)),
        check_vma=False,
    )
```

```python
import jax
import jax.numpy as jnp
from jax import lax
from jax.sharding import Mesh, PartitionSpec as P

AXES = ("t", "z", "x", "y", "c")
DP = ("z", "x", "y", "c")


def swap(x, axis, mask=1):
    return lax.ppermute(x, axis, [(i, i ^ mask) for i in range(lax.axis_size(axis))])


def row_scales(sums, squares, width):
    average = sums / width
    return average, lax.rsqrt(squares / width - average * average + 1e-06)


def normed(values, average, inverse, gain):
    values = values.astype(jnp.float32)
    return ((values - average) * inverse * gain[None, :]).astype(jnp.bfloat16)


def rounded(x):
    return lax.reduce_precision(x, 8, 7)


def columns_of(vectors, count=128):
    column = lax.broadcasted_iota(jnp.int32, (vectors[0].shape[0], count), 1)
    block = jnp.zeros(column.shape, jnp.float32)
    for i, rest in enumerate(vectors):
        for k in range(3):
            piece = rounded(rest)
            block = jnp.where(column == 3 * i + k, piece[:, None], block)
            rest = rest - piece
    return block.astype(jnp.bfloat16)


def vector_of(block, i):
    return jnp.sum(block[:, 3 * i : 3 * i + 3].astype(jnp.float32), axis=1, keepdims=True)


def float16_rows(*parts):
    column = lax.broadcasted_iota(jnp.int32, (parts[0].shape[0], 128), 1)
    exponents = jnp.zeros(column.shape, jnp.float32)
    scaled = []
    for i, part in enumerate(parts):
        square = jnp.mean(part * part, axis=1, keepdims=True)
        exponent = jnp.round(0.5 * jnp.log2(square + 1e-30))
        exponents = jnp.where(column == i, exponent, exponents)
        scaled.append(part * jnp.exp2(-exponent))
    return jnp.concatenate(scaled + [exponents], axis=1).astype(jnp.float16)


def from_float16(rows, width):
    exponents = rows[:, 2 * width :].astype(jnp.float32)
    return [
        rows[:, i * width : (i + 1) * width].astype(jnp.float32) * jnp.exp2(exponents[:, i : i + 1])
        for i in range(2)
    ]


def packed_rows(projected, average, inverse):
    length = jnp.sqrt(jnp.sum(projected * projected, axis=1, keepdims=True) + 1e-06)
    unit = (projected / length).astype(jnp.bfloat16)
    return jnp.concatenate([unit, columns_of([length[:, 0], average, inverse])], axis=1)


def tied(*arrays):
    return lax.optimization_barrier(arrays)


def gather_rows(text, image, text_2, image_4):
    low, high = jnp.split(text, 2, axis=0)
    image_z = [swap(image, "z", k) for k in (1, 2, 3)]
    low_1, high_1, near, text_2b = tied(
        swap(low, "x", 1), swap(high, "y", 1), image_z[0], swap(text_2, "x", 3)
    )
    text_4 = jnp.concatenate([text_2, text_2b], axis=0)
    image_y = [swap(image, "y", 3), swap(near, "y", 3)]
    low, high = jnp.concatenate([low, low_1], axis=0), jnp.concatenate([high, high_1], axis=0)
    low_1, high_1, text_4b, *image_z = tied(
        swap(low, "x", 3), swap(high, "x", 1), swap(text_4, "y", 1), *image_z[1:]
    )
    text_8 = jnp.concatenate([text_4, text_4b], axis=0)
    far = jnp.concatenate(image_z, axis=0)
    low, high = jnp.concatenate([low, low_1], axis=0), jnp.concatenate([high, high_1], axis=0)
    low_1, high_1, image_4, *image_y = tied(
        swap(low, "y", 1), swap(high, "x", 3), image_4, *image_y, swap(far, "y", 3)
    )
    text = both_cores(jnp.concatenate([low, low_1, high, high_1], axis=0))
    image = jnp.concatenate([image, near, far] + image_y, axis=0)
    return text, image, text_8, jnp.concatenate([image_4, swap(image_4, "y", 3)], axis=0)


def both_cores(x):
    return jnp.concatenate([x, swap(x, "c")], axis=0)


def by_index(parts, axis):
    index = lax.axis_index(axis)
    even, low = index % 2 == 0, index < 2
    pairs = [
        [jnp.where(even, a, b), jnp.where(even, b, a)] for a, b in (parts[:2], parts[2:])
    ]
    return [jnp.where(low, a, b) for a, b in zip(*pairs)] + [
        jnp.where(low, b, a) for a, b in zip(*pairs)
    ]


def gather_xy(block):
    parts = [part[None, None] for part in jnp.split(block, 2, axis=0)]
    for axes in (("x", "y"), ("y", "x")):
        others = tied(
            *[swap(part, axis, k) for k in (2, 1, 3) for part, axis in zip(parts, axes)]
        )
        parts = [
            jnp.concatenate(
                by_index([part, others[2 + i], others[i], others[4 + i]], axis),
                axis=("x", "y").index(axis),
            )
            for i, (part, axis) in enumerate(zip(parts, axes))
        ]
    parts = [part.reshape((-1,) + part.shape[2:]) for part in parts]
    return jnp.concatenate(parts, axis=1)


def slope(gradient, packed, width):
    unit = packed[:, :width].astype(jnp.float32)
    length = vector_of(packed[:, width:], 0)
    along = jnp.sum(unit * gradient, axis=1, keepdims=True)
    value = (gradient - unit * along) / length
    high = rounded(value)
    return high.astype(jnp.bfloat16), (value - high).astype(jnp.bfloat16)


def over_rows(features, slopes):
    return sum(
        lax.dot_general(
            features, part, (((0,), (0,)), ((), ())), preferred_element_type=jnp.float32
        )
        for part in slopes
    )


def per_device(image_x, text_x, image_gain, text_gain, image_w, text_w, sharpness, offset):
    scale, bias = sharpness[0], offset[0]
    towers = lax.axis_size("t")
    rows, width = image_x.shape[0], image_w.shape[1]
    image_values = image_x.astype(jnp.float32)
    text_values = text_x.astype(jnp.float32)
    moments = lax.psum(
        (
            jnp.sum(image_values, axis=1),
            jnp.sum(image_values * image_values, axis=1),
            jnp.sum(text_values, axis=1),
            jnp.sum(text_values * text_values, axis=1),
        ),
        "t",
    )
    moments, *image_z = tied(moments, *[swap(image_x, "z", k) for k in (1, 2, 3)])
    image_4 = jnp.concatenate([image_x] + image_z, axis=0)
    image_scales = row_scales(moments[0], moments[1], image_x.shape[1] * towers)
    text_scales = row_scales(moments[2], moments[3], text_x.shape[1] * towers)
    image_part = jnp.dot(
        normed(image_x, *[v[:, None] for v in image_scales], image_gain),
        image_w,
        preferred_element_type=jnp.float32,
    )
    text_part = jnp.dot(
        normed(text_x, *[v[:, None] for v in text_scales], text_gain),
        text_w,
        preferred_element_type=jnp.float32,
    )
    send, text_0 = tied(float16_rows(image_part, text_part), text_x)
    other, text_1 = tied(swap(send, "t"), swap(text_0, "x", 1))
    image_other, text_other = from_float16(other, width)
    text_rows, image_rows, text_8, image_features = gather_rows(
        packed_rows(text_part + text_other, *text_scales),
        packed_rows(image_part + image_other, *image_scales),
        jnp.concatenate([text_x, text_1], axis=0),
        image_4,
    )
    chips = text_8.reshape(2, 2, 2, 2, rows // 2, text_x.shape[1])
    text_features = both_cores(
        jnp.concatenate(
            [
                chips[:, :, :, 0].reshape(-1, text_x.shape[1]),
                chips[:, :, :, 1].transpose(1, 2, 0, 3, 4).reshape(-1, text_x.shape[1]),
            ],
            axis=0,
        )
    )
    image_normed_rows, text_normed_rows = (
        normed(features, vector_of(block, 1), vector_of(block, 2), gain)
        for features, block, gain in (
            (image_features, image_rows[:, width:], image_gain),
            (text_features, text_rows[:, width:], text_gain),
        )
    )

    image_units, text_units = image_rows[:, :width], text_rows[:, :width]
    products = lax.dot_general(
        image_units, text_units, (((1,), (1,)), ((), ())), preferred_element_type=jnp.float32
    )
    logits = scale * products + bias
    half = rows // 2
    row_ids = lax.broadcasted_iota(jnp.int32, products.shape, 0)
    column_ids = lax.broadcasted_iota(jnp.int32, products.shape, 1)
    same = ((column_ids == row_ids) & (row_ids < half)) | (
        (column_ids == row_ids + 7 * half) & (row_ids >= half) & (row_ids < rows)
    )
    labels = jnp.where(same, 1.0, -1.0).astype(jnp.float32)
    weights = (-labels * jax.nn.sigmoid(-labels * logits)).astype(jnp.bfloat16)
    image_grad = scale * jnp.dot(weights, text_units, preferred_element_type=jnp.float32)
    text_grad = scale * lax.dot_general(
        weights, image_units, (((0,), (0,)), ((), ())), preferred_element_type=jnp.float32
    )
    image_slope = slope(image_grad, image_rows, width)
    text_slope = slope(text_grad, text_rows, width)
    first = lax.axis_index("c") == 0

    def over_cores(term):
        lower, upper = jnp.split(term, 2, axis=0)
        return jnp.where(first, lower, upper) + swap(jnp.where(first, upper, lower), "c")

    image_kept = over_cores(over_rows(image_normed_rows, image_slope))
    text_kept = over_cores(over_rows(text_normed_rows, text_slope))
    plane = lax.axis_size("x") * lax.axis_size("y")
    image_deep, text_deep = image_w.shape[0] // 2, text_w.shape[0] // 2
    deep = image_deep + text_deep
    each = -(-deep // (plane * 16)) * 16
    kept = jnp.concatenate(
        [image_kept, text_kept, jnp.zeros((plane * each - deep, width), jnp.float32)], axis=0
    )
    blocks = kept.astype(jnp.bfloat16).reshape(plane, each, width)
    blocks = lax.all_to_all(blocks, ("x", "y"), 0, 0)
    block = rounded(jnp.sum(blocks.astype(jnp.float32), axis=0))
    others = tied(*[swap(block.astype(jnp.bfloat16), "z", k) for k in (2, 3, 1)])
    z2, z3, z1 = [other.astype(jnp.float32) for other in others]
    block = ((block + z1) + (z2 + z3)).astype(jnp.bfloat16)
    block = gather_xy(block).reshape(plane * each, width)
    other = swap(block, "c")
    lower, upper = jnp.where(first, block, other), jnp.where(first, other, block)
    return tuple(
        jnp.concatenate([lower[rows], upper[rows]], axis=0).astype(jnp.float32)
        for rows in (slice(0, image_deep), slice(image_deep, deep))
    )


def solution(mesh):
    grid = Mesh(mesh.devices.reshape(2, 4, 4, 4, 2), AXES)
    return jax.shard_map(
        per_device,
        mesh=grid,
        in_specs=(
            P(DP, "t"),
            P(DP, "t"),
            P("t"),
            P("t"),
            P("t", None),
            P("t", None),
            P(),
            P(),
        ),
        out_specs=(P("t", None), P("t", None)),
        check_vma=False,
    )
```
